256 devices in a mesh: dp: 32 (over z, y), expert: 8 (over x, core).
Axes of the slice: x: 4, y: 4, z: 8, core: 2. Of those that a mesh axis runs over, the one named last changes fastest.
Arguments:
- tokens: bfloat16 [128, 32, 2048], P('dp'), may hold values from -20 to 20
- memory: bfloat16 [128, 32, 2048], P('dp', None, 'expert'), may hold values from -128 to 128
- source_length: int32 [128], P('dp'), may hold values from 1 to 32, 3072 in all
- owner_device: int32 [128], P('dp'), may hold values from 0 to 31, as said below
- source_device: int32 [128], P('dp'), may hold values from 0 to 31, as said below
- target_length: int32 [128], P('dp'), may hold values from 1 to 32, 3072 in all
- routing: int32 [128, 32, 2], P('dp'), may hold values from 0 to 31, all different within a row; in each aligned block of 128 rows (0 to 127, 128 to 255, ..., all dimensions but the last counted through in order) at most 16 rows name the same one
- attn_gain: float32 [2048], replicated, may hold values from 0.5 to 1.5
- ffn_gain: float32 [2048], replicated, may hold values from 0.5 to 1.5
- query_weight: bfloat16 [2048, 1024], P(None, 'expert'), may hold values from -1 to 1
- key_weight: bfloat16 [2048, 1024], P(None, 'expert'), may hold values from -1 to 1
- value_weight: bfloat16 [2048, 1024], P(None, 'expert'), may hold values from -0.125 to 0.125
- out_weight: bfloat16 [1024, 2048], P('expert'), may hold values from -0.1875 to 0.1875
- router_weight: bfloat16 [2048, 32], replicated, may hold values from -1 to 1
- up_weight: bfloat16 [32, 2048, 4096], P('dp', None, 'expert'), may hold values from -0.125 to 0.125
- down_weight: bfloat16 [32, 4096, 2048], P('dp', 'expert'), may hold values from -0.09375 to 0.09375
- grad_out: bfloat16 [128, 32, 2048], P('dp'), may hold values from -6 to 6
Outputs:
- memory_grad: bfloat16 [128, 32, 2048], P('dp', None, 'expert')
- up_grad: bfloat16 [32, 2048, 4096], P('dp', None, 'expert')
- down_grad: bfloat16 [32, 4096, 2048], P('dp', 'expert')
The draws below stay inside these ranges and needn't reach their ends.
Inputs may be any that keep to these rules, and one draw needn't show every extreme that they name: Source sentence k of dp index i goes to position k of dp index owner_device[i * 4 + k]; for every k the sentences in position k of all dp indices go to all dp indices, one to each; one dp index sends at most one sentence to any other dp index. The inverse of owner_device: target position k of dp index j holds source sentence k of dp index source_device[j * 4 + k]. `routing`: among the 128 tokens of one dp index, at most 16 (token, choice) pairs name the same expert.
All inputs are finite; a program needn't handle non-finite values. No bound on the sum of `source_length` or of `target_length` on one device may be relied on, other than what follows from the above.
Results may differ from the reference program's by a relative error of at most 0.035.
The reference program's roundings to bfloat16 on the way count: a program that leaves them out, or rounds other values in their place, can miss the bound.
Values may be sent and summed in bfloat16 or wider, within the bound.
A program may use at most 64 MiB of HBM per device.

```python
import math
import jax
import jax.numpy as jnp
import numpy as np
from jax import lax

D = 2048
FF_WINDOW = 4096
HEADS = 8
HEAD_DIM = 128
SENT_DEV = 4
TGT_LEN = 32
SRC_LEN = 32
SENTENCES = 128
EXPERTS = 32
CAP = 16
N_DP = 32
N_EXPERT = 8


def sentence_plans(key):
    first_key, second_key = jax.random.split(key)
    order_first = jax.random.permutation(first_key, N_DP).astype(jnp.int32)
    order_second = jax.random.permutation(second_key, N_DP).astype(jnp.int32)
    inverse_first = jnp.argsort(order_first, stable=True).astype(jnp.int32)
    inverse_second = jnp.argsort(order_second, stable=True).astype(jnp.int32)
    device_rows = jnp.arange(N_DP, dtype=jnp.int32)[:, None]
    position = jnp.arange(SENT_DEV, dtype=jnp.int32)[None, :]
    owners = order_second[(order_first[device_rows] + position) % N_DP]
    sources = inverse_first[(inverse_second[device_rows] - position) % N_DP]
    return (owners.reshape(-1).astype(jnp.int32), sources.reshape(-1).astype(jnp.int32))


def common_direction(key):
    return jnp.clip(jax.random.normal(jax.random.fold_in(key, 102), (D,), jnp.float32), -4.0, 4.0)


def token_parts(key, common_scale):
    noise_rows = jnp.clip(jax.random.normal(jax.random.fold_in(key, 101), (SENTENCES, TGT_LEN, D), jnp.float32), -4.0, 4.0)
    direction = common_direction(key)
    row_scale = common_scale * jax.random.uniform(jax.random.fold_in(key, 103), (SENTENCES, TGT_LEN), jnp.float32)
    sentence = jnp.arange(SENTENCES, dtype=jnp.int32)[:, None]
    position = jnp.arange(TGT_LEN, dtype=jnp.int32)[None, :]
    planted = jnp.logical_and(sentence % 4 == 0, position == 0)
    row_scale = jnp.where(planted, 0.0, row_scale)
    return noise_rows + row_scale[:, :, None] * direction[None, None, :]


def projection_base(key):
    return jnp.clip(jax.random.normal(jax.random.fold_in(key, 104), (D, HEADS * HEAD_DIM), jnp.float32), -4.0, 4.0) / math.sqrt(D)


def draw_owner_device(key, part):
    return sentence_plans(key)[0]


def draw_source_device(key, part):
    return sentence_plans(key)[1]


def draw_tokens(key, part):
    common_scale = 0.0
    return token_parts(key, common_scale).astype(jnp.bfloat16)


def draw_memory(key, part):
    key = jax.random.fold_in(key, 7)
    memory_rows = jnp.clip(jax.random.normal(key, (SENTENCES, SRC_LEN, D), jnp.float32), -6.0, 6.0)
    return memory_rows.astype(jnp.bfloat16)


def draw_query_weight(key, part):
    return projection_base(key).astype(jnp.bfloat16)


def draw_key_weight(key, part):
    key = jax.random.fold_in(key, 13)
    fresh = jnp.clip(jax.random.normal(key, (D, HEADS * HEAD_DIM), jnp.float32), -4.0, 4.0) / math.sqrt(D)
    return fresh.astype(jnp.bfloat16)


def draw_router_weight(key, part):
    key = jax.random.fold_in(key, 17)
    columns = jnp.clip(jax.random.normal(key, (D, EXPERTS), jnp.float32), -4.0, 4.0) / math.sqrt(D)
    return columns.astype(jnp.bfloat16)


def block_scale(key, extent, cuts, least, largest):
    factor_of, own = 1.0, jax.random.fold_in(key, 6)
    for dim, shards_of in cuts:
        draws = jnp.exp(jax.random.uniform(jax.random.fold_in(own, dim), (shards_of,), jnp.float32, least / len(cuts), largest / len(cuts)))
        factor_of = factor_of * jnp.repeat(draws, extent[dim] // shards_of).reshape([-1 if axis == dim else 1 for axis in range(len(extent))])
    return factor_of


def split_up(number_of, total, limit, slope):
    portions = [(1 << 20) // math.isqrt(grade ** slope) + 1 for grade in range(2, number_of + 1)]
    surplus, given = total - limit - (number_of - 1), [1] * (number_of - 1)
    while surplus > 0:
        candidates = [i for i in range(number_of - 1) if given[i] < limit]
        pool, budget = sum([portions[i] for i in candidates]), surplus
        for i in candidates:
            addition = min(limit - given[i], max(1, budget * portions[i] // pool), surplus)
            given[i] = given[i] + addition
            surplus = surplus - addition
    return np.array([limit] + given)


def uneven_parts(own_key, amount, total, reach, slope):
    if amount == 2:
        one = jax.random.randint(own_key, (), max(1, total - reach), min(reach, total - 1) + 1)
        return jnp.stack([one, total - one])
    sizes = jnp.asarray(split_up(amount, total, reach, slope), jnp.int32)
    twos = (amount - 1) // 2
    donor, receiver = sizes[1:1 + 2 * twos:2], sizes[2:2 + 2 * twos:2]
    margin = jnp.minimum(donor - 1, reach - receiver)
    passed = jax.random.randint(jax.random.fold_in(own_key, 1), (twos,), 0, 1 << 20) % (margin + 1)
    sizes = sizes.at[1:1 + 2 * twos:2].set(donor - passed).at[2:2 + 2 * twos:2].set(receiver + passed)
    return sizes[jax.random.permutation(jax.random.fold_in(own_key, 2), amount)]


def routed_block(stream_key, own, number, rows, number_of, top, reach, slope):
    order = jax.random.permutation(stream_key, number_of)
    heavy_load, common = portions_of(number_of, rows * top, reach, slope, True), portions_of(number_of, rows * top, reach, slope, False)
    places = jnp.arange(number_of)

    def named(tallies, offset_by):
        used = int((tallies > 0).sum())
        fixed = max(1, used // 4)
        passed = fixed + (places - fixed + offset_by * (used - fixed)) % max(1, number_of - fixed)
        return jnp.zeros((number_of,), jnp.int32).at[order[jnp.where(places < fixed, places, passed)]].set(jnp.asarray(tallies, jnp.int32))

    tallies = jnp.where(number % 4 == 0, named(heavy_load, number // 4), named(common, number - number // 4 - 1))
    mixed = jax.random.permutation(jax.random.fold_in(own, 3), number_of)
    source_of, sink = mixed[0:number_of // 2 * 2:2], mixed[1:number_of // 2 * 2:2]
    room = jnp.minimum(tallies[source_of] - 1, reach - tallies[sink]) // 2
    room = jnp.where((source_of == order[0]) | (sink == order[0]) | (tallies[sink] == 0), 0, jnp.maximum(room, 0))
    passed = jax.random.randint(jax.random.fold_in(own, 4), (number_of // 2,), 0, 1 << 20) % (room + 1)
    tallies = tallies.at[source_of].add(-passed).at[sink].add(passed)
    items = jnp.searchsorted(jnp.cumsum(tallies), jnp.arange(rows * top), side="right").astype(jnp.int32)
    table = items.reshape(top, rows).T
    table = table[jax.random.permutation(jax.random.fold_in(own, 1), rows)]
    offset_by = jax.random.randint(jax.random.fold_in(own, 2), (rows, 1), 0, top)
    return jnp.take_along_axis(table, (jnp.arange(top)[None, :] + offset_by) % top, axis=1)


def portions_of(number_of, total, bound, slope, full):
    portions = [(1 << 20) // math.isqrt(rank ** slope) + 1 for rank in range(1, number_of + 1)]
    largest = bound if full else min(bound, max(-(-total // number_of), total * portions[0] // sum(portions)))
    least = 1 if total - largest >= number_of - 1 else 0
    counts, spare = [largest] + [least] * (number_of - 1), total - largest - least * (number_of - 1)
    while spare > 0:
        candidates = [i for i in range(1, number_of) if counts[i] < largest] or [i for i in range(1, number_of) if counts[i] < bound]
        whole, budget = sum([portions[i] for i in candidates]), spare
        for i in candidates:
            addition = min(bound - counts[i], max(1, budget * portions[i] // whole), spare)
            counts[i] = counts[i] + addition
            spare = spare - addition
    return np.array(counts)


def bell_draw(key, extent, deviation, bound, shards=(), held_as=jnp.bfloat16):
    values = jax.random.normal(key, extent, jnp.float32) * deviation
    if len(shards) > 0:
        values = block_scale(key, extent, shards, -0.22, 0.18) * values
    return jnp.clip(values, min=-bound, max=bound).astype(held_as)


def setup_inputs(seed: int = 0) -> dict:
    seeds = jax.random.split(jax.random.key(seed), 18)
    tokens = draw_tokens(jax.random.fold_in(seeds[17], 71), 0)
    memory = draw_memory(jax.random.fold_in(seeds[17], 71), 0)
    source_length = uneven_parts(seeds[2], SENTENCES, SENTENCES * SRC_LEN * 3 // 4, SRC_LEN, 2).astype(jnp.int32)
    owner_device = draw_owner_device(jax.random.fold_in(seeds[17], 71), 0)
    source_device = draw_source_device(jax.random.fold_in(seeds[17], 71), 0)
    target_length = uneven_parts(seeds[5], SENTENCES, SENTENCES * TGT_LEN * 3 // 4, TGT_LEN, 2).astype(jnp.int32)
    routing_keys = jax.random.split(jax.random.fold_in(seeds[6], 1), SENTENCES * TGT_LEN // (SENT_DEV * TGT_LEN))
    routing_turns = jax.random.permutation(jax.random.fold_in(seeds[6], 3), SENTENCES * TGT_LEN // (SENT_DEV * TGT_LEN))
    routing = jax.vmap(lambda own, number: routed_block(jax.random.fold_in(seeds[6], 2), own, number, SENT_DEV * TGT_LEN, EXPERTS, 2, CAP, 2))(routing_keys, routing_turns).reshape((SENTENCES, TGT_LEN, 2))
    attn_gain = jnp.clip(1.0 + 0.1 * jax.random.normal(seeds[7], (D,), jnp.float32), 0.5, 1.5)
    ffn_gain = jnp.clip(1.0 + 0.1 * jax.random.normal(seeds[8], (D,), jnp.float32), 0.5, 1.5)
    query_weight = draw_query_weight(jax.random.fold_in(seeds[17], 71), 0)
    key_weight = draw_key_weight(jax.random.fold_in(seeds[17], 71), 0)
    value_weight = bell_draw(seeds[11], (D, HEADS * HEAD_DIM), D ** -0.5, 0.125, ((1, 8),))
    out_weight = bell_draw(seeds[12], (HEADS * HEAD_DIM, D), (HEADS * HEAD_DIM) ** -0.5, 0.1875, ((0, 8),))
    router_weight = draw_router_weight(jax.random.fold_in(seeds[17], 71), 0)
    up_weight = bell_draw(seeds[14], (EXPERTS, D, FF_WINDOW), D ** -0.5, 0.125, ((0, 32), (2, 8)))
    down_weight = bell_draw(seeds[15], (EXPERTS, FF_WINDOW, D), FF_WINDOW ** -0.5, 0.09375, ((0, 32), (1, 8)))
    grad_out = bell_draw(seeds[16], (SENTENCES, TGT_LEN, D), 1.0, 6.0, ((0, 32),))
    return dict(tokens=tokens, memory=memory, source_length=source_length, owner_device=owner_device, source_device=source_device, target_length=target_length, routing=routing, attn_gain=attn_gain, ffn_gain=ffn_gain, query_weight=query_weight, key_weight=key_weight, value_weight=value_weight, out_weight=out_weight, router_weight=router_weight, up_weight=up_weight, down_weight=down_weight, grad_out=grad_out)


def layer_norm(values, norm_gain):
    average = lax.optimization_barrier(jnp.mean(values, axis=-1, keepdims=True))
    centered = values - average
    variance = lax.optimization_barrier(jnp.mean(centered * centered, axis=-1, keepdims=True))
    return centered * lax.rsqrt(variance + 1e-05) * norm_gain

def gate_from_logits(logits, routing_rows):
    chances = jax.nn.softmax(logits, axis=-1)
    chosen = (routing_rows[:, :, None] == jnp.arange(logits.shape[1], dtype=jnp.int32)[None, None, :]).astype(jnp.float32)
    picked = jnp.einsum('rce,re->rc', chosen, chances, precision=lax.Precision.HIGHEST)
    return picked / lax.optimization_barrier(jnp.sum(picked, axis=-1, keepdims=True))

def router_back(logit_grad, router_weight):
    high_part = logit_grad.astype(jnp.bfloat16)
    low_part = (logit_grad - high_part.astype(jnp.float32)).astype(jnp.bfloat16)
    return jnp.dot(high_part, router_weight.T, preferred_element_type=jnp.float32) + jnp.dot(low_part, router_weight.T, preferred_element_type=jnp.float32)

def slot_ranks(routing_rows, expert_count):
    pair_expert = routing_rows.reshape(-1)
    matches = (pair_expert[:, None] == jnp.arange(expert_count, dtype=jnp.int32)[None, :]).astype(jnp.int32)
    ranked = lax.optimization_barrier(jnp.sum(jnp.cumsum(matches, axis=0) * matches, axis=1)) - 1
    return ranked.reshape(routing_rows.shape).astype(jnp.int32)

def attend(queries, key_heads, value_heads, key_length):
    scaling = queries.shape[-1] ** (-0.5)
    scores = jnp.einsum('sqhd,skhd->shqk', queries.astype(jnp.float32), key_heads.astype(jnp.float32)) * scaling
    key_open = jnp.arange(key_heads.shape[1], dtype=jnp.int32)[None, :] < key_length[:, None]
    scores = jnp.where(key_open[:, None, None, :], scores, -1e+30)
    probabilities = jax.nn.softmax(scores, axis=-1)
    weights = probabilities.astype(jnp.bfloat16)
    attended = jnp.einsum('shqk,skhd->sqhd', weights.astype(jnp.float32), value_heads.astype(jnp.float32)).astype(jnp.bfloat16)
    return (attended, probabilities, weights)

def attend_back(queries, key_heads, value_heads, probabilities, weights, attended_grad):
    scaling = queries.shape[-1] ** (-0.5)
    grad_f = attended_grad.astype(jnp.float32)
    value_grad = jnp.einsum('shqk,sqhd->skhd', weights.astype(jnp.float32), grad_f).astype(jnp.bfloat16)
    prob_grad = jnp.einsum('sqhd,skhd->shqk', grad_f, value_heads.astype(jnp.float32))
    score_grad = (probabilities * (prob_grad - lax.optimization_barrier(jnp.sum(probabilities * prob_grad, axis=-1, keepdims=True))) * scaling).astype(jnp.bfloat16)
    key_grad = jnp.einsum('shqk,sqhd->skhd', score_grad.astype(jnp.float32), queries.astype(jnp.float32)).astype(jnp.bfloat16)
    return (key_grad, value_grad)

def block_sum(terms):
    rounded = lax.optimization_barrier(terms.astype(jnp.bfloat16))
    return lax.optimization_barrier(jnp.sum(rounded.astype(jnp.float32), axis=0)).astype(jnp.bfloat16)

def expert_forward(slots_in, up_slice, down_slice):
    slot_total = slots_in.shape[0]
    block_width = FF_WINDOW // N_EXPERT
    pre_act = jnp.dot(slots_in, up_slice, preferred_element_type=jnp.float32)
    activation = jax.nn.gelu(pre_act).astype(jnp.bfloat16)
    block_act = activation.reshape(slot_total, N_EXPERT, block_width).astype(jnp.float32)
    block_down = down_slice.reshape(N_EXPERT, block_width, D).astype(jnp.float32)
    return block_sum(jnp.einsum('rjf,jfd->jrd', block_act, block_down))

def expert_backward(slots_in, out_grad, up_slice, down_slice):
    slot_total = slots_in.shape[0]
    block_width = FF_WINDOW // N_EXPERT
    pre_act = jnp.dot(slots_in, up_slice, preferred_element_type=jnp.float32)
    activation = jax.nn.gelu(pre_act).astype(jnp.bfloat16)
    down_grad = jnp.dot(activation.T, out_grad, preferred_element_type=jnp.float32).astype(jnp.bfloat16)
    act_grad = jnp.dot(out_grad, down_slice.T, preferred_element_type=jnp.float32)
    pre_grad = jax.vjp(jax.nn.gelu, pre_act)[1](act_grad)[0].astype(jnp.bfloat16)
    up_grad = jnp.dot(slots_in.T, pre_grad, preferred_element_type=jnp.float32).astype(jnp.bfloat16)
    block_grad = pre_grad.reshape(slot_total, N_EXPERT, block_width).astype(jnp.float32)
    block_up = up_slice.reshape(D, N_EXPERT, block_width).astype(jnp.float32)
    input_slots = block_sum(jnp.einsum('rjf,djf->jrd', block_grad, block_up))
    return (up_grad, down_grad, input_slots)

def reference(tokens, memory, source_length, owner_device, source_device, target_length, routing, attn_gain, ffn_gain, query_weight, key_weight, value_weight, out_weight, router_weight, up_weight, down_weight, grad_out):
    position = jnp.arange(SENT_DEV, dtype=jnp.int32)[None, :]
    source_grid = source_device.reshape(N_DP, SENT_DEV)
    owner_grid = owner_device.reshape(N_DP, SENT_DEV)
    arrived = memory.reshape(N_DP, SENT_DEV, SRC_LEN, D)[source_grid, position].reshape(SENTENCES * SRC_LEN, D)
    key_length = source_length.reshape(N_DP, SENT_DEV)[source_grid, position].reshape(SENTENCES)
    token_rows = SENTENCES * TGT_LEN
    flat_tokens = tokens.reshape(token_rows, D)
    normed = layer_norm(flat_tokens.astype(jnp.float32), attn_gain).astype(jnp.bfloat16)
    queries = jnp.dot(normed, query_weight, preferred_element_type=jnp.float32).astype(jnp.bfloat16).reshape(SENTENCES, TGT_LEN, HEADS, HEAD_DIM)
    key_heads = jnp.dot(arrived, key_weight, preferred_element_type=jnp.float32).astype(jnp.bfloat16).reshape(SENTENCES, SRC_LEN, HEADS, HEAD_DIM)
    value_heads = jnp.dot(arrived, value_weight, preferred_element_type=jnp.float32).astype(jnp.bfloat16).reshape(SENTENCES, SRC_LEN, HEADS, HEAD_DIM)
    attended, probabilities, weights = attend(queries, key_heads, value_heads, key_length)
    attended_rows = attended.reshape(token_rows, HEADS * HEAD_DIM)
    hidden = (flat_tokens.astype(jnp.float32) + jnp.dot(attended_rows, out_weight, preferred_element_type=jnp.float32)).astype(jnp.bfloat16)
    expert_in = layer_norm(hidden.astype(jnp.float32), ffn_gain).astype(jnp.bfloat16)
    routing_rows = routing.reshape(token_rows, 2)
    logits = jnp.dot(expert_in, router_weight, preferred_element_type=jnp.float32)
    gate_shares = gate_from_logits(logits, routing_rows)
    block_rows = SENT_DEV * TGT_LEN
    route_blocks = routing.reshape(N_DP, block_rows, 2)
    ranks = jax.vmap(lambda packed: slot_ranks(packed, EXPERTS))(route_blocks)
    block_ids = jnp.broadcast_to(jnp.arange(N_DP, dtype=jnp.int32)[:, None, None], route_blocks.shape)

    def to_slots(pair_values, filler):
        return filler.at[route_blocks, block_ids, ranks].set(pair_values)
    pairs_in = jnp.broadcast_to(expert_in.reshape(N_DP, block_rows, 1, D), (N_DP, block_rows, 2, D))
    slots_in = to_slots(pairs_in, jnp.zeros((EXPERTS, N_DP, CAP, D), jnp.bfloat16)).reshape(EXPERTS, N_DP * CAP, D)
    expert_out = lax.map(lambda packed: expert_forward(*packed), (slots_in, up_weight, down_weight))
    target_live = jnp.arange(TGT_LEN, dtype=jnp.int32)[None, :] < target_length[:, None]
    live_grad = jnp.where(target_live[:, :, None], grad_out, jnp.zeros((), jnp.bfloat16)).reshape(token_rows, D)
    pairs_grad = jnp.broadcast_to(live_grad.reshape(N_DP, block_rows, 1, D), (N_DP, block_rows, 2, D))
    grad_slots = to_slots(pairs_grad, jnp.zeros((EXPERTS, N_DP, CAP, D), jnp.bfloat16))
    gate_slots = to_slots(gate_shares.reshape(N_DP, block_rows, 2), jnp.zeros((EXPERTS, N_DP, CAP), jnp.float32))
    slot_gate_grad = lax.optimization_barrier(jnp.sum(expert_out.reshape(EXPERTS, N_DP, CAP, D).astype(jnp.float32) * grad_slots.astype(jnp.float32), axis=-1))
    gate_grad = slot_gate_grad[route_blocks, block_ids, ranks].reshape(token_rows, 2)
    out_grad = (grad_slots.astype(jnp.float32) * gate_slots[..., None]).astype(jnp.bfloat16).reshape(EXPERTS, N_DP * CAP, D)
    up_grad, down_grad, input_slots = lax.map(lambda packed: expert_backward(*packed), (slots_in, out_grad, up_weight, down_weight))
    input_grad = input_slots.reshape(EXPERTS, N_DP, CAP, D)[route_blocks, block_ids, ranks].reshape(token_rows, 2, D).astype(jnp.float32)
    ffn_in_grad = lax.optimization_barrier(jnp.sum(gate_shares[:, :, None] * input_grad, axis=1))
    logit_grad = jax.vjp(lambda inputs: gate_from_logits(inputs, routing_rows), logits)[1](gate_grad)[0]
    ffn_in_grad = ffn_in_grad + router_back(logit_grad, router_weight)
    norm_back = jax.vjp(lambda inputs: layer_norm(inputs, ffn_gain), hidden.astype(jnp.float32))[1]
    hidden_grad = (live_grad.astype(jnp.float32) + norm_back(ffn_in_grad)[0]).astype(jnp.bfloat16)
    attended_grad = jnp.dot(hidden_grad, out_weight.T, preferred_element_type=jnp.float32).astype(jnp.bfloat16).reshape(SENTENCES, TGT_LEN, HEADS, HEAD_DIM)
    key_grad, value_grad = attend_back(queries, key_heads, value_heads, probabilities, weights, attended_grad)
    arrived_grad = jnp.dot(key_grad.reshape(SENTENCES * SRC_LEN, HEADS * HEAD_DIM), key_weight.T, preferred_element_type=jnp.float32)
    arrived_grad = arrived_grad + jnp.dot(value_grad.reshape(SENTENCES * SRC_LEN, HEADS * HEAD_DIM), value_weight.T, preferred_element_type=jnp.float32)
    arrived_grad = arrived_grad.astype(jnp.bfloat16).reshape(N_DP, SENT_DEV, SRC_LEN, D)
    memory_grad = arrived_grad[owner_grid, position].reshape(SENTENCES, SRC_LEN, D)
    return (memory_grad, up_grad, down_grad)
```

```python
import functools

import jax
import jax.numpy as jnp
from jax import lax
from jax.experimental import pallas as pl
from jax.experimental.pallas import tpu as pltpu
from jax.sharding import PartitionSpec as P

F32 = jnp.float32
BF16 = jnp.bfloat16
HI = lax.Precision.HIGHEST
LANES = 128
CAP = 16
TILE = 16
GROUPS = 4
EPS = 1e-5


def dot(a, b, ca=1, cb=0, precision=None):
    return lax.dot_general(
        a, b, (((ca,), (cb,)), ((), ())), preferred_element_type=F32, precision=precision
    )


def iota(shape, dim):
    return lax.broadcasted_iota(jnp.int32, shape, dim)


def log2(value):
    return value.bit_length() - 1


def to_rows(columns):
    rows = columns[0].shape[0]
    lane = iota((rows, LANES), 1)
    packed = jnp.zeros((rows, LANES), F32)
    for i, column in enumerate(columns):
        packed = jnp.where(lane == i, column, packed)
    return packed.T[:8]


def to_columns(rows, count):
    padded = jnp.concatenate([rows, jnp.zeros((LANES - 8, rows.shape[1]), F32)], axis=0).T
    return [padded[:, i : i + 1] for i in range(count)]


def stack_rows(*rows):
    fill = jnp.zeros((8 - len(rows), rows[0].shape[1]), F32)
    return jnp.concatenate([*rows, fill], axis=0)


class Layout:
    def __init__(self, n_dp, n_e, sentences, length, width, head, hidden, experts):
        self.n_dp, self.n_e, self.n_x = n_dp, n_e, n_e // 2
        self.S, self.L, self.T = sentences, length, sentences * length
        self.D, self.F = width, width // n_e
        self.Hd, self.H, self.E = head, hidden, experts
        self.R = n_dp * CAP
        self.mids = n_dp // 2
        self.gs = n_dp // GROUPS
        self.Q = self.R // GROUPS


def layer_kernel(
    z,
    src_ref, slen_ref, tlen_ref, routing_ref, again_ref, fgain_ref,
    tokens_hbm, memory_hbm, grad_hbm, wq_hbm, wk_hbm, wv_hbm, wo_hbm, wr_hbm, up_hbm, down_hbm,
    mem_out, up_out, down_out,
    tok, live, wq, wk, wv, wo, wr, up, down,
    mem_all, ow_all, att_all, hg_all, x_all, g_all,
    g_send, x_send, ret_send, ret_recv,
    meta, kv_send, mid_buf, mid_out_buf, kv_recv, kvg_send, mid_buf2, mid_out2, kvg_recv,
    stat1, stat2, lg_all, gate_send, gate_recv, gg_all, gg_send, gg_recv,
    plan, plan0, plan1, relay_plan, u_buf, act_buf, pg_buf,
    sib_send, sib_recv, pair, xs_send, far_recv, lft_recv, rgt_recv,
    m_sib_send, m_sib_recv, m_pair, m_xs_send, m_far_recv, m_lft_recv, m_rgt_recv,
    ug, dg, mg, hid,
    ss, rs, ls,
):
    n_dp, n_e, T, D, F, R, Q = z.n_dp, z.n_e, z.T, z.D, z.F, z.R, z.Q
    me = lax.axis_index("dp")
    e = lax.axis_index("expert")
    x, c = e // 2, e % 2
    xr, xl = (x + 1) % 4, (x + 3) % 4
    sib = 2 * x + (1 - c)
    right, left = 2 * xr + c, 2 * xl + c
    my_group = me // z.gs
    col_e = pl.multiple_of(e * F, F)

    counter = [0]

    def sems(count):
        first = counter[0]
        counter[0] += count
        return first

    def copy(src, dst, k, dp, ex, ks=None):
        return pltpu.make_async_remote_copy(
            src_ref=src,
            dst_ref=dst,
            send_sem=ss.at[k if ks is None else ks],
            recv_sem=rs.at[k],
            device_id=(dp, ex),
            device_id_type=pl.DeviceIdType.MESH,
        )

    pending = []

    def send(src, dst, k, dp, ex):
        copy(src, dst, k, dp, ex).start()
        pending.append(lambda: copy(src, dst, k, dp, ex).wait_send())

    def arrive(dst, k):
        copy(dst, dst, k, me, sib).wait_recv()

    def rows16(ref, i):
        return ref.at[pl.ds(pl.multiple_of(i * CAP, CAP), CAP)]

    def one_row(ref, i):
        return ref.at[pl.ds(i, 1)]

    class Spread:
        def __init__(self, src, dst):
            self.src, self.dst = src, dst
            self.base = sems(n_dp)

        def one(self, t):
            return copy(self.src(t), self.dst(me), self.base + me, t, e, ks=self.base + t)

        def start(self):
            def step(kk, carry):
                group = (my_group + kk // z.gs) % GROUPS
                t = group * z.gs + (me % z.gs + kk % z.gs) % z.gs
                self.one(t).start()
                return carry

            lax.fori_loop(1, n_dp, step, 0)

            def finish():
                def step(kk, carry):
                    self.one((me + kk) % n_dp).wait_send()
                    return carry

                lax.fori_loop(1, n_dp, step, 0)

            pending.append(finish)

        def start_group(self, group):
            def step(kk, carry):
                t = group * z.gs + (me % z.gs + kk) % z.gs

                @pl.when(t != me)
                def _():
                    self.one(t).start()

                return carry

            lax.fori_loop(0, z.gs, step, 0)

        def finish_later(self):
            def finish():
                def step(kk, carry):
                    self.one((me + kk) % n_dp).wait_send()
                    return carry

                lax.fori_loop(1, n_dp, step, 0)

            pending.append(finish)

        def wait_group(self, group):
            def step(kk, carry):
                i = group * z.gs + kk

                @pl.when(i != me)
                def _():
                    arrive(self.dst(i), self.base + i)

                return carry

            lax.fori_loop(0, z.gs, step, 0)

        def wait(self):
            def step(kk, carry):
                i = (me + n_dp - kk) % n_dp
                arrive(self.dst(i), self.base + i)
                return carry

            lax.fori_loop(1, n_dp, step, 0)

    class Gather:
        def __init__(self, part, parts):
            self.part, self.parts = part, parts
            self.base = sems(7 * parts)

        def go(self, q, t, block, peer):
            ref = self.part(block, q)
            send(ref, ref, self.base + 7 * q + t, me, peer)

        def got(self, q, t, block):
            arrive(self.part(block, q), self.base + 7 * q + t)

        def start(self, q):
            self.go(q, 0, e, right)
            self.go(q, 1, e, left)
            self.go(q, 2, e, sib)

        def mid(self, q):
            self.got(q, 0, left)
            if q % 2 == 0:
                self.go(q, 6, left, right)
            self.go(q, 3, left, sib)
            self.got(q, 1, right)
            if q % 2 == 1:
                self.go(q, 6, right, left)
            self.go(q, 4, right, sib)

        def far(self, q):
            across = 2 * ((x + 2) % 4) + c
            self.got(q, 6, across)
            self.go(q, 5, across, sib)

        def end(self, q):
            other = 1 - c
            self.got(q, 2, 2 * x + other)
            self.got(q, 3, 2 * xl + other)
            self.got(q, 4, 2 * xr + other)
            self.got(q, 5, 2 * ((x + 2) % 4) + other)

        def whole(self):
            for step in (self.start, self.mid, self.far, self.end):
                for q in range(self.parts):
                    step(q)

    class Exchange:
        def __init__(self, src, dst):
            self.src, self.dst = src, dst
            self.base = sems(n_e)

        def start(self):
            for p in range(1, n_e):
                peer = 2 * ((x + p // 2) % 4) + (c + p % 2) % 2
                send(self.src(peer), self.dst(e), self.base + p, me, peer)

        def wait(self):
            for p in range(1, n_e):
                peer = 2 * ((x + 4 - p // 2) % 4) + (c + p % 2) % 2
                arrive(self.dst(peer), self.base + p)

    class Reduce:
        def __init__(self, first, n, partial, bufs):
            self.n, self.half, self.partial = n, n // 2, partial
            self.first = first
            self.sib_send, self.sib_recv, self.pair, self.xs, self.far, self.lft, self.rgt = bufs
            self.base = sems(10)

        def rows(self, ref, lead, half=None):
            if half is None:
                piece = pl.ds(pl.multiple_of(self.first, TILE), self.n)
            else:
                piece = pl.ds(pl.multiple_of(self.first + half * self.half, TILE), self.half)
            return ref.at[piece] if lead is None else ref.at[lead, piece]

        def local(self):
            for i, dx in enumerate((2, 1, 3, 0)):
                block = 2 * ((x + dx) % 4) + (1 - c)
                mine = self.rows(self.sib_send, dx)
                mine[...] = self.partial(block).astype(BF16)
                send(mine, self.rows(self.sib_recv, dx), self.base + dx, me, sib)

        def put(self, dx, half, extra, target, landing, t):
            value = self.rows(self.pair, dx, half)[...]
            if extra is not None:
                value = value + extra[...].astype(F32)
            out = self.rows(self.xs, dx, half)
            out[...] = value.astype(BF16)
            send(out, self.rows(landing, None, half), self.base + t, me, target)

        def pairs(self):
            for dx in (2, 1, 3, 0):
                block = 2 * ((x + dx) % 4) + c
                own = self.partial(block)
                theirs = self.rows(self.sib_recv, dx)
                arrive(theirs, self.base + dx)
                self.rows(self.pair, dx)[...] = own + theirs[...].astype(F32)
                if dx == 2:
                    self.put(2, 0, None, right, self.far, 4)
                    self.put(2, 1, None, left, self.far, 5)
                elif dx == 1:
                    self.put(1, 1, None, right, self.lft, 6)
                elif dx == 3:
                    self.put(3, 0, None, left, self.rgt, 7)

        def relay(self):
            arrived = self.rows(self.far, None, 0)
            arrive(arrived, self.base + 4)
            self.put(1, 0, arrived, right, self.lft, 8)
            arrived = self.rows(self.far, None, 1)
            arrive(arrived, self.base + 5)
            self.put(3, 1, arrived, left, self.rgt, 9)

        def total(self):
            arrive(self.rows(self.lft, None, 1), self.base + 6)
            arrive(self.rows(self.rgt, None, 0), self.base + 7)
            arrive(self.rows(self.lft, None, 0), self.base + 8)
            arrive(self.rows(self.rgt, None, 1), self.base + 9)
            return (
                self.rows(self.pair, 0)[...]
                + self.rows(self.lft, None)[...].astype(F32)
                + self.rows(self.rgt, None)[...].astype(F32)
            )

    local = {}

    def load(name, src, dst):
        copy_in = pltpu.make_async_copy(src, dst, ls.at[len(local)])
        copy_in.start()
        local[name] = copy_in

    load("memory", memory_hbm, mem_all.at[e])
    load("grad", grad_hbm.at[:, pl.ds(col_e, F)], live)
    load("wo", wo_hbm, wo)
    load("tokens", tokens_hbm, tok)
    load("wq", wq_hbm, wq)
    load("wk", wk_hbm, wk)
    load("wv", wv_hbm, wv)
    load("wr", wr_hbm.at[pl.ds(pl.multiple_of(e * F, F), F)], wr)
    load("down", down_hbm, down)
    load("up", up_hbm, up)

    barrier = pltpu.get_barrier_semaphore()

    def greet(kk, carry):
        pl.semaphore_signal(
            barrier, inc=1, device_id=((me + kk) % n_dp, e), device_id_type=pl.DeviceIdType.MESH
        )
        return carry

    lax.fori_loop(1, n_dp, greet, 0)
    for p in range(1, n_e):
        pl.semaphore_signal(
            barrier, inc=1, device_id=(me, (e + p) % n_e), device_id_type=pl.DeviceIdType.MESH
        )

    routing = routing_ref[...]
    choice = [routing[:, 0:1], routing[:, 1:2]]
    lane_te = iota((T, LANES), 1)
    hot = [(lane_te == choice[i]).astype(F32) for i in range(2)]
    before = (iota((T, T), 0) > iota((T, T), 1)).astype(BF16)
    counts = dot(before, (hot[0] + hot[1]).astype(BF16))
    rank = [jnp.sum(hot[i] * counts, axis=1, keepdims=True) for i in range(2)]
    slot = [choice[i].astype(F32) * CAP + rank[i] for i in range(2)]
    names = to_rows([choice[0].astype(F32), choice[1].astype(F32), rank[0], rank[1], slot[0], slot[1]])
    names = names.astype(jnp.int32)
    slot_row = iota((R, T), 0)
    plan[...] = jnp.logical_or(slot_row == names[4:5], slot_row == names[5:6]).astype(BF16)
    slot_lane = iota((T, R), 1)
    plan0[...] = (slot_lane == slot[0].astype(jnp.int32)).astype(BF16)
    plan1[...] = (slot_lane == slot[1].astype(jnp.int32)).astype(BF16)

    lane_1 = iota((1, LANES), 1)
    note = jnp.zeros((1, LANES), jnp.int32)
    for k in range(z.S):
        note = jnp.where(lane_1 == k, src_ref[k], note)
        note = jnp.where(lane_1 == z.S + k, slen_ref[k], note)
    meta[pl.ds(me, 1), :] = note.astype(F32)

    local["grad"].wait()
    row_t = iota((T, 1), 0)
    length = jnp.zeros((T, 1), jnp.int32)
    for k in range(z.S):
        length = jnp.where((row_t >> log2(z.L)) == k, tlen_ref[k], length)
    alive = (row_t & (z.L - 1)) < length
    live[...] = jnp.where(alive, live[...].astype(F32), 0.0).astype(BF16)
    slots = dot(plan[...], live[...]).astype(BF16)
    g_send[...] = slots
    own_rows = pl.ds(pl.multiple_of(me * CAP, CAP), CAP)
    g_all[e, own_rows, :] = g_send[own_rows, :]

    pl.semaphore_wait(barrier, n_dp - 1 + n_e - 1)

    def halves(ref, rows):
        return lambda b, q: ref.at[b, pl.ds(q * (rows // 2), rows // 2)]

    local["memory"].wait()
    memory_gather = Gather(halves(mem_all, T), 2)
    memory_gather.start(0)
    memory_gather.start(1)
    meta_spread = Spread(lambda t: one_row(meta, me), lambda i: one_row(meta, i))
    meta_spread.start()
    g_spread = Spread(lambda t: rows16(g_send, t), lambda i: rows16(g_all.at[e], i))
    g_spread.start()

    local["tokens"].wait()
    local["wq"].wait()
    rows_f = tok[...].astype(F32)
    centred = rows_f - jnp.mean(rows_f, axis=1, keepdims=True)
    variance = jnp.mean(centred * centred, axis=1, keepdims=True)
    normed = (centred * lax.rsqrt(variance + EPS) * again_ref[...]).astype(BF16)
    queries = dot(normed, wq[...]).astype(BF16)

    for q in range(2):
        memory_gather.mid(q)
    local["wo"].wait()
    for b in range(n_e):

        @pl.when(e == b)
        def _():
            ow_all[b] = wo[:, b * F : (b + 1) * F]

    ow_exchange = Exchange(
        lambda peer: wo.at[:, pl.ds(pl.multiple_of(peer * F, F), F)], lambda b: ow_all.at[b]
    )
    for q in range(2):
        memory_gather.far(q)
    for q in range(2):
        memory_gather.end(q)
    ow_exchange.start()

    local["wk"].wait()
    local["wv"].wait()
    keys = jnp.zeros((T, z.Hd), F32)
    values = jnp.zeros((T, z.Hd), F32)
    for b in range(n_e):
        block = mem_all[b]
        keys = keys + dot(block, wk[b * F : (b + 1) * F, :])
        values = values + dot(block, wv[b * F : (b + 1) * F, :])

    r_out = iota((2 * T, 2 * T), 0)
    r_in = iota((2 * T, 2 * T), 1)
    place = (
        ((r_out >> 3) & 1) * T + ((r_out >> 1) & 3) * z.L + ((r_out >> 4) << 1) + (r_out & 1)
    )
    order = (r_in == place).astype(BF16)

    middle_me = me % 2 == (me // 4 + c) % 2
    my_middle = me // 2

    def middle_dp(m):
        return 2 * m + (m // 2 + c) % 2

    class Relay:
        def __init__(self, send_buf, held, sorted_buf, recv_buf):
            self.send_buf, self.held, self.sorted_buf, self.recv_buf = (
                send_buf, held, sorted_buf, recv_buf,
            )
            self.out = sems(n_dp)
            self.back = sems(n_dp)

        def first(self, m):
            return copy(
                rows16(self.send_buf, m), rows16(self.held, me), self.out + me, middle_dp(m), e,
                ks=self.out + m,
            )

        def second(self, j):
            return copy(
                rows16(self.sorted_buf, j), rows16(self.recv_buf, my_middle),
                self.back + my_middle, j, e, ks=self.back + j,
            )

        def each_middle(self, action):
            def step(kk, carry):
                m = (my_middle + kk) % z.mids

                @pl.when(middle_dp(m) != me)
                def _():
                    action(m)

                return carry

            lax.fori_loop(0, z.mids, step, 0)

        def each_other(self, action):
            def step(kk, carry):
                action((me + kk) % n_dp)
                return carry

            lax.fori_loop(1, n_dp, step, 0)

        def start(self):
            self.each_middle(lambda m: self.first(m).start())

            @pl.when(middle_me)
            def _():
                rows16(self.held, me)[...] = rows16(self.send_buf, my_middle)[...]

        def turn(self, transposed):
            @pl.when(middle_me)
            def _():
                self.each_other(lambda i: arrive(rows16(self.held, i), self.out + i))
                self.sorted_buf[...] = dot(
                    relay_plan[...], self.held[...], 0 if transposed else 1, 0
                ).astype(BF16)
                self.each_other(lambda j: self.second(j).start())
                rows16(self.recv_buf, my_middle)[...] = rows16(self.sorted_buf, me)[...]

        def end(self):
            self.each_middle(lambda m: arrive(rows16(self.recv_buf, m), self.back + m))

        def finish(self):
            self.each_middle(lambda m: self.first(m).wait_send())

            @pl.when(middle_me)
            def _():
                self.each_other(lambda j: self.second(j).wait_send())

    both = jnp.concatenate([keys.astype(BF16), values.astype(BF16)], axis=0)
    kv_send[...] = dot(order, both).astype(BF16)
    relay = Relay(kv_send, mid_buf, mid_out_buf, kv_recv)
    relay.start()

    meta_spread.wait()
    notes = meta[...]
    span = n_dp * TILE
    pick = ((iota((span, n_dp), 0) >> 4) == iota((span, n_dp), 1)).astype(BF16)
    spread_notes = dot(pick, notes.astype(BF16))
    wanted = ((iota((span, LANES), 0) >> 1) & 3) == iota((span, LANES), 1)
    source = jnp.sum(jnp.where(wanted, spread_notes, 0.0), axis=1, keepdims=True).astype(jnp.int32)
    p_row = iota((span, span), 0)
    p_col = iota((span, span), 1)
    relay_plan[...] = (p_col == (source * TILE + (p_row & (TILE - 1)))).astype(BF16)
    relay.turn(False)

    g_spread.wait()
    g_gather = Gather(halves(g_all, R), 2)
    g_gather.start(0)
    g_gather.start(1)

    key_length = jnp.zeros((1, T), F32)
    key_at = iota((1, T), 1)
    n_row, n_lane = iota((n_dp, LANES), 0), iota((n_dp, LANES), 1)
    for k in range(z.S):
        here = jnp.logical_and(n_row == src_ref[k], n_lane == z.S + k)
        found = jnp.sum(jnp.where(here, notes, 0.0), axis=1, keepdims=True)
        found = jnp.sum(found, axis=0, keepdims=True)
        key_length = jnp.where((key_at >> log2(z.L)) == k, found, key_length)

    relay.end()
    kv = dot(order, kv_recv[...], 0, 0).astype(BF16)
    key_heads, value_heads = kv[:T], kv[T:]

    scaling = z.Hd ** (-0.5)
    same = (iota((T, T), 0) >> log2(z.L)) == (iota((T, T), 1) >> log2(z.L))
    inside = (key_at & (z.L - 1)).astype(F32) < key_length
    open_keys = jnp.logical_and(same, inside)
    scores = jnp.where(open_keys, dot(queries, key_heads, 1, 1) * scaling, -1e30)
    exps = jnp.exp(scores - jnp.max(scores, axis=1, keepdims=True))
    probabilities = exps / jnp.sum(exps, axis=1, keepdims=True)
    weights = probabilities.astype(BF16)
    att_all[e] = dot(weights, value_heads).astype(BF16)
    att_gather = Gather(halves(att_all, T), 2)
    for q in range(2):
        att_gather.start(q)
    for q in range(2):
        att_gather.mid(q)
    for q in range(2):
        att_gather.far(q)
    for q in range(2):
        g_gather.mid(q)
    ow_exchange.wait()
    for q in range(2):
        att_gather.end(q)

    heads_sum = jnp.zeros((T, F), F32)
    for b in range(n_e):
        heads_sum = heads_sum + dot(att_all[b], ow_all[b])
    hidden = (tok[:, pl.ds(col_e, F)].astype(F32) + heads_sum).astype(BF16).astype(F32)
    hid[...] = hidden
    part_sum = jnp.sum(hidden, axis=1, keepdims=True)
    off = hidden - part_sum * (1.0 / F)
    part_sq = jnp.sum(off * off, axis=1, keepdims=True)
    stat1[e] = to_rows([part_sum, part_sq])
    stat1_exchange = Exchange(lambda peer: stat1.at[e], lambda b: stat1.at[b])
    stat1_exchange.start()
    for q in range(2):
        g_gather.far(q)
    for q in range(2):
        g_gather.end(q)
    stat1_exchange.wait()
    parts = [stat1[b] for b in range(n_e)]
    mean_row = sum(p[0:1] for p in parts) * (1.0 / D)
    square_row = sum(p[1:2] for p in parts)
    for p in parts:
        shift = p[0:1] * (1.0 / F) - mean_row
        square_row = square_row + F * (shift * shift)
    rstd_row = lax.rsqrt(square_row * (1.0 / D) + EPS)
    mean, rstd = to_columns(stack_rows(mean_row, rstd_row), 2)
    gain = fgain_ref[:, pl.ds(col_e, F)]
    unit = (hidden - mean) * rstd
    expert_in = (unit * gain).astype(BF16)

    x_send[...] = dot(plan[...], expert_in).astype(BF16)
    x_all[e, own_rows, :] = x_send[own_rows, :]
    x_spread = Spread(lambda t: rows16(x_send, t), lambda i: rows16(x_all.at[e], i))
    x_spread.start()
    local["wr"].wait()
    router = wr[...]
    logit_part = dot(expert_in, router)
    wide = jnp.concatenate([logit_part, jnp.zeros((T, LANES - z.E), F32)], axis=1)
    lg_all[e] = wide.T[: z.E]
    lg_exchange = Exchange(lambda peer: lg_all.at[e], lambda b: lg_all.at[b])
    lg_exchange.start()

    local["down"].wait()

    def down_back(q, carry):
        piece = pl.ds(pl.multiple_of(q * Q, Q), Q)
        total = jnp.zeros((Q, z.H), F32)
        for b in range(n_e):
            total = total + dot(g_all[b, piece, :], down[:, b * F : (b + 1) * F], 1, 1)
        u_buf[piece, :] = total
        return carry

    lax.fori_loop(0, 2, down_back, 0)

    lg_exchange.wait()
    logits = sum(lg_all[b] for b in range(n_e))
    expert_row = iota((z.E, T), 0)
    hot_rows = [expert_row == names[i : i + 1] for i in range(2)]
    chosen = [jnp.sum(jnp.where(h, logits, 0.0), axis=0, keepdims=True) for h in hot_rows]
    top = jnp.maximum(chosen[0], chosen[1])
    lifted = [jnp.exp(v - top) for v in chosen]
    share = [v / (lifted[0] + lifted[1]) for v in lifted]
    rank_lane = [
        (iota((T, LANES), 1) == rank[i].astype(jnp.int32)).astype(F32) for i in range(2)
    ]
    gate_rows = jnp.zeros((z.E, LANES), F32)
    for i in range(2):
        gate_rows = gate_rows + dot(jnp.where(hot_rows[i], share[i], 0.0), rank_lane[i], 1, 0, HI)
    gate_send[...] = gate_rows
    gate_recv[pl.ds(me, 1), :] = gate_send[pl.ds(me, 1), :]
    gate_spread = Spread(lambda t: one_row(gate_send, t), lambda i: one_row(gate_recv, i))
    gate_spread.start()
    lax.fori_loop(2, GROUPS, down_back, 0)

    def group_first(k):
        return ((my_group + GROUPS - k) % GROUPS) * Q

    x_gather = Gather(lambda b, k: x_all.at[b, pl.ds(pl.multiple_of(group_first(k), Q), Q)], GROUPS)
    local["up"].wait()
    reduces = []

    def expert_group(k):
        first = group_first(k)
        piece = pl.ds(pl.multiple_of(first, Q), Q)
        pre = jnp.zeros((Q, z.H), F32)
        for b in range(n_e):
            pre = pre + dot(x_all[b, piece, :], up[b * F : (b + 1) * F, :])
        cubic = pre * pre * pre
        slope_in = 0.7978845608028654 * (pre + 0.044715 * cubic)
        bend = jnp.tanh(slope_in)
        act = (pre * (0.5 * (1.0 + bend))).astype(BF16)
        act_buf[piece, :] = act
        slope = 0.5 * (1.0 + bend) + 0.5 * pre * (1.0 - bend * bend) * (
            0.7978845608028654 * (1.0 + 3.0 * 0.044715 * pre * pre)
        )
        grads = u_buf[piece, :]
        gates, pick, wanted = gate_column(first, Q)
        pg_buf[piece, :] = (gates * grads * slope).astype(BF16)
        dots = jnp.sum(act.astype(F32) * grads, axis=1, keepdims=True)
        return dot(pick, jnp.where(wanted, dots, 0.0), 0, 0, HI)

    def gate_column(first, rows):
        pick = (((iota((rows, n_dp), 0) + first) >> 4) == iota((rows, n_dp), 1)).astype(F32)
        wanted = (iota((rows, LANES), 0) & (CAP - 1)) == iota((rows, LANES), 1)
        spread_gates = dot(pick, gate_recv[...], 1, 0, HI)
        gates = jnp.sum(jnp.where(wanted, spread_gates, 0.0), axis=1, keepdims=True)
        return gates, pick, wanted

    def input_partial(first):
        def partial(block):
            piece = pl.ds(pl.multiple_of(first, Q), Q)
            rows = pl.ds(pl.multiple_of(block * F, F), F)
            return dot(pg_buf[piece, :], up[rows, :], 1, 1)

        return partial

    ret_spread = Spread(lambda t: rows16(ret_send, t), lambda i: rows16(ret_recv, i))
    ret_spread.finish_later()
    bufs = (sib_send, sib_recv, pair, xs_send, far_recv, lft_recv, rgt_recv)

    def give_back(k):
        first = group_first(k)
        piece = pl.ds(pl.multiple_of(first, Q), Q)
        ret_send[piece, :] = reduces[k].total().astype(BF16)
        ret_spread.start_group((my_group + GROUPS - k) % GROUPS)

    gg_total = jnp.zeros((n_dp, LANES), F32)
    for step in range(GROUPS + 3):
        if step < GROUPS:
            x_spread.wait_group((my_group + GROUPS - step) % GROUPS)
            x_gather.start(step)
        if 1 <= step < GROUPS + 1:
            x_gather.mid(step - 1)
        if 2 <= step < GROUPS + 2:
            x_gather.far(step - 2)
        if step == 2:
            gate_spread.wait()
        if step >= 3:
            k = step - 3
            x_gather.end(k)
            gg_total = gg_total + expert_group(k)
            reduces.append(Reduce(group_first(k), Q, input_partial(group_first(k)), bufs))
            reduces[k].local()
            reduces[k].pairs()
            if k >= 1:
                reduces[k - 1].relay()

    gg_all[e] = gg_total
    gg_exchange = Exchange(lambda peer: gg_all.at[e], lambda b: gg_all.at[b])
    gg_exchange.start()
    reduces[GROUPS - 1].relay()

    def up_back(b, carry):
        rows = pl.ds(pl.multiple_of(b * F, F), F)
        ug[rows, :] = dot(x_all[b], pg_buf[...], 0, 0).astype(BF16)
        return carry

    gates_all = gate_column(0, R)[0]

    def down_grad(b, carry):
        columns = pl.ds(pl.multiple_of(b * F, F), F)
        scaled = (g_all[b].astype(F32) * gates_all).astype(BF16)
        dg[:, columns] = dot(act_buf[...], scaled, 0, 0).astype(BF16)
        return carry

    give_back(0)
    gg_exchange.wait()
    gg_sum = sum(gg_all[b] for b in range(n_e))
    gg_send[...] = gg_sum
    gg_recv[pl.ds(me, 1), :] = gg_send[pl.ds(me, 1), :]
    gg_spread = Spread(lambda t: one_row(gg_send, t), lambda i: one_row(gg_recv, i))
    gg_spread.start()
    give_back(1)
    lax.fori_loop(0, n_e // 2, up_back, 0)
    give_back(2)
    lax.fori_loop(n_e // 2, n_e, up_back, 0)
    give_back(3)
    ret_recv[own_rows, :] = ret_send[own_rows, :]
    up_store = pltpu.make_async_copy(ug, up_out, ls.at[len(local)])
    up_store.start()
    lax.fori_loop(0, n_e // 2, down_grad, 0)

    gg_spread.wait()
    gate_grad = []
    for i in range(2):
        spread_gg = dot(gg_recv[...], rank_lane[i], 1, 1, HI)
        gate_grad.append(jnp.sum(jnp.where(hot_rows[i], spread_gg, 0.0), axis=0, keepdims=True))
    delta = share[0] * share[1] * (gate_grad[0] - gate_grad[1])
    logit_grad = jnp.where(hot_rows[0], delta, 0.0) - jnp.where(hot_rows[1], delta, 0.0)
    high = logit_grad.astype(BF16)
    low = (logit_grad - high.astype(F32)).astype(BF16)
    router_term = dot(high, router, 0, 1) + dot(low, router, 0, 1)
    share_columns = to_columns(stack_rows(share[0], share[1]), 2)

    ret_spread.wait()
    returned = ret_recv[...]
    ffn_in_grad = (
        share_columns[0] * dot(plan0[...], returned)
        + share_columns[1] * dot(plan1[...], returned)
        + router_term
    )

    scaled_in = ffn_in_grad * gain
    unit = (hid[...] - mean) * rstd
    stat2[e] = to_rows(
        [
            jnp.sum(scaled_in, axis=1, keepdims=True),
            jnp.sum(scaled_in * unit, axis=1, keepdims=True),
        ]
    )
    stat2_exchange = Exchange(lambda peer: stat2.at[e], lambda b: stat2.at[b])
    stat2_exchange.start()
    lax.fori_loop(n_e // 2, n_e, down_grad, 0)
    down_store = pltpu.make_async_copy(dg, down_out, ls.at[len(local) + 1])
    down_store.start()
    stat2_exchange.wait()
    sums = sum(stat2[b] for b in range(n_e)) * (1.0 / D)
    mean_in, mean_unit = to_columns(sums, 2)
    hidden_grad = live[...].astype(F32) + rstd * (scaled_in - mean_in - unit * mean_unit)
    hg_all[e] = hidden_grad.astype(BF16)
    hg_gather = Gather(halves(hg_all, T), 2)
    hg_gather.whole()

    att_grad = jnp.zeros((T, z.Hd), F32)
    for b in range(n_e):
        att_grad = att_grad + dot(hg_all[b], wo[:, b * F : (b + 1) * F], 1, 1)
    att_grad = att_grad.astype(BF16)
    value_grad = dot(weights, att_grad, 0, 0).astype(BF16)
    prob_grad = dot(att_grad, value_heads, 1, 1)
    inner = jnp.sum(probabilities * prob_grad, axis=1, keepdims=True)
    score_grad = (probabilities * (prob_grad - inner) * scaling).astype(BF16)
    key_grad = dot(score_grad, queries, 0, 0).astype(BF16)
    both = jnp.concatenate([key_grad, value_grad], axis=0)
    kvg_send[...] = dot(order, both).astype(BF16)
    relay_back = Relay(kvg_send, mid_buf2, mid_out2, kvg_recv)
    relay_back.start()
    relay_back.turn(True)
    relay_back.end()
    home = dot(order, kvg_recv[...], 0, 0).astype(BF16)
    home_keys, home_values = home[:T], home[T:]

    def memory_partial(block):
        rows = pl.ds(pl.multiple_of(block * F, F), F)
        return dot(home_keys, wk[rows, :], 1, 1) + dot(home_values, wv[rows, :], 1, 1)

    memory_reduce = Reduce(
        0, T, memory_partial,
        (m_sib_send, m_sib_recv, m_pair, m_xs_send, m_far_recv, m_lft_recv, m_rgt_recv),
    )
    memory_reduce.local()
    memory_reduce.pairs()
    memory_reduce.relay()
    mg[...] = memory_reduce.total().astype(BF16)
    mem_store = pltpu.make_async_copy(mg, mem_out, ls.at[len(local) + 2])
    mem_store.start()

    relay.finish()
    relay_back.finish()
    for finish in pending:
        finish()
    up_store.wait()
    down_store.wait()
    mem_store.wait()
    assert counter[0] <= SEMS, counter[0]


SEMS = 512


def build(mesh):
    n_dp, n_e = mesh.shape["dp"], mesh.shape["expert"]

    def body(
        tokens, memory, source_length, owner_device, source_device, target_length, routing,
        attn_gain, ffn_gain, query_weight, key_weight, value_weight, out_weight, router_weight,
        up_weight, down_weight, grad_out,
    ):
        sentences, length, width = tokens.shape
        z = Layout(
            n_dp, n_e, sentences, length, width, query_weight.shape[1], up_weight.shape[2],
            router_weight.shape[1],
        )
        T, D, F, R, H = z.T, z.D, z.F, z.R, z.H
        span = n_dp * TILE
        vm = pltpu.VMEM
        scratch = [
            vm((T, D), BF16), vm((T, F), BF16), vm((D, z.Hd), BF16), vm((D, z.Hd), BF16),
            vm((D, z.Hd), BF16), vm((z.Hd, D), BF16), vm((F, z.E), BF16), vm((D, H), BF16),
            vm((H, D), BF16),
            vm((n_e, T, F), BF16), vm((n_e, z.Hd, F), BF16), vm((n_e, T, z.Hd), BF16),
            vm((n_e, T, F), BF16), vm((n_e, R, F), BF16), vm((n_e, R, F), BF16),
            vm((R, F), BF16), vm((R, F), BF16), vm((R, F), BF16), vm((R, F), BF16),
            vm((n_dp, LANES), F32),
            vm((2 * T, z.Hd), BF16), vm((span, z.Hd), BF16), vm((span, z.Hd), BF16),
            vm((2 * T, z.Hd), BF16),
            vm((2 * T, z.Hd), BF16), vm((span, z.Hd), BF16), vm((span, z.Hd), BF16),
            vm((2 * T, z.Hd), BF16),
            vm((n_e, 8, T), F32), vm((n_e, 8, T), F32), vm((n_e, z.E, T), F32),
            vm((z.E, LANES), F32), vm((n_dp, LANES), F32), vm((n_e, n_dp, LANES), F32),
            vm((n_dp, LANES), F32), vm((n_dp, LANES), F32),
            vm((R, T), BF16), vm((T, R), BF16), vm((T, R), BF16), vm((span, span), BF16),
            vm((R, H), F32), vm((R, H), BF16), vm((R, H), BF16),
            vm((4, R, F), BF16), vm((4, R, F), BF16), vm((4, R, F), F32), vm((4, R, F), BF16),
            vm((R, F), BF16), vm((R, F), BF16), vm((R, F), BF16),
            vm((4, T, F), BF16), vm((4, T, F), BF16), vm((4, T, F), F32), vm((4, T, F), BF16),
            vm((T, F), BF16), vm((T, F), BF16), vm((T, F), BF16),
            vm((D, H), BF16), vm((H, D), BF16), vm((T, F), BF16), vm((T, F), F32),
            pltpu.SemaphoreType.DMA((SEMS,)), pltpu.SemaphoreType.DMA((SEMS,)),
            pltpu.SemaphoreType.DMA((16,)),
        ]
        smem = pl.BlockSpec(memory_space=pltpu.SMEM)
        vmem = pl.BlockSpec(memory_space=pltpu.VMEM)
        hbm = pl.BlockSpec(memory_space=pl.ANY)
        mem_grad, up_grad, down_grad = pl.pallas_call(
            functools.partial(layer_kernel, z),
            out_shape=(
                jax.ShapeDtypeStruct((T, F), BF16),
                jax.ShapeDtypeStruct((D, H), BF16),
                jax.ShapeDtypeStruct((H, D), BF16),
            ),
            in_specs=[smem] * 3 + [vmem] * 3 + [hbm] * 10,
            out_specs=(hbm, hbm, hbm),
            scratch_shapes=scratch,
            compiler_params=pltpu.CompilerParams(
                collective_id=0, has_side_effects=True, vmem_limit_bytes=56 * 1024 * 1024
            ),
            name="layer",
        )(
            source_device, source_length, target_length, routing.reshape(T, 2),
            attn_gain[None], ffn_gain[None],
            tokens.reshape(T, D), memory.reshape(T, F), grad_out.reshape(T, D),
            query_weight, key_weight, value_weight, out_weight, router_weight,
            up_weight[0], down_weight[0],
        )
        return mem_grad.reshape(sentences, length, F), up_grad[None], down_grad[None]

    return body


def solution(mesh):
    in_specs = (
        P("dp", None, None),
        P("dp", None, "expert"),
        P("dp"),
        P("dp"),
        P("dp"),
        P("dp"),
        P("dp", None, None),
        P(),
        P(),
        P(None, "expert"),
        P(None, "expert"),
        P(None, "expert"),
        P("expert", None),
        P(),
        P("dp", None, "expert"),
        P("dp", "expert", None),
        P("dp", None, None),
    )
    out_specs = (P("dp", None, "expert"), P("dp", None, "expert"), P("dp", "expert", None))
    return jax.shard_map(
        build(mesh), mesh=mesh, in_specs=in_specs, out_specs=out_specs, check_vma=False
    )
```

```python
import functools

import jax
import jax.numpy as jnp
from jax import lax
from jax.experimental import pallas as pl
from jax.experimental.pallas import tpu as pltpu
from jax.sharding import PartitionSpec as P

F32 = jnp.float32
BF16 = jnp.bfloat16
HI = lax.Precision.HIGHEST
LANES = 128
CAP = 16
TILE = 16
GROUPS = 4
EPS = 1e-5


def dot(a, b, ca=1, cb=0, precision=None):
    return lax.dot_general(
        a, b, (((ca,), (cb,)), ((), ())), preferred_element_type=F32, precision=precision
    )


def iota(shape, dim):
    return lax.broadcasted_iota(jnp.int32, shape, dim)


def log2(value):
    return value.bit_length() - 1


def to_rows(columns):
    rows = columns[0].shape[0]
    lane = iota((rows, LANES), 1)
    packed = jnp.zeros((rows, LANES), F32)
    for i, column in enumerate(columns):
        packed = jnp.where(lane == i, column, packed)
    return packed.T[:8]


def to_columns(rows, count):
    padded = jnp.concatenate([rows, jnp.zeros((LANES - 8, rows.shape[1]), F32)], axis=0).T
    return [padded[:, i : i + 1] for i in range(count)]


def stack_rows(*rows):
    fill = jnp.zeros((8 - len(rows), rows[0].shape[1]), F32)
    return jnp.concatenate([*rows, fill], axis=0)


class Layout:
    def __init__(self, n_dp, n_e, sentences, length, width, head, hidden, experts):
        self.n_dp, self.n_e, self.n_x = n_dp, n_e, n_e // 2
        self.S, self.L, self.T = sentences, length, sentences * length
        self.D, self.F = width, width // n_e
        self.Hd, self.H, self.E = head, hidden, experts
        self.R = n_dp * CAP
        self.mids = n_dp // 2
        self.gs = n_dp // GROUPS
        self.Q = self.R // GROUPS


def layer_kernel(
    z,
    src_ref, slen_ref, tlen_ref, routing_ref, again_ref, fgain_ref,
    tokens_hbm, memory_hbm, grad_hbm, wq_hbm, wk_hbm, wv_hbm, wo_hbm, wr_hbm, up_hbm, down_hbm,
    mem_out, up_out, down_out,
    tok, live, wq, wk, wv, wo, wr, up, down,
    mem_all, ow_all, att_all, hg_all, x_all, g_all,
    g_send, x_send, ret_send, ret_recv,
    meta, kv_send, mid_buf, mid_out_buf, kv_recv, kvg_send, mid_buf2, mid_out2, kvg_recv,
    stat1, stat2, lg_all, gate_send, gate_recv, gg_all, gg_send, gg_recv,
    plan, plan0, plan1, relay_plan, u_buf, act_buf, pg_buf,
    sib_send, sib_recv, own_sum, xs_send, xs_recv, uw_send, uw_recv, mg_send, mg_recv,
    ug, dg, mg, hid,
    ss, rs, ls,
):
    n_dp, n_e, T, D, F, R, Q = z.n_dp, z.n_e, z.T, z.D, z.F, z.R, z.Q
    me = lax.axis_index("dp")
    e = lax.axis_index("expert")
    x, c = e // 2, e % 2
    xr, xl = (x + 1) % 4, (x + 3) % 4
    sib = 2 * x + (1 - c)
    right, left = 2 * xr + c, 2 * xl + c
    across = 2 * ((x + 2) % 4) + c
    my_group = me // z.gs
    col_e = pl.multiple_of(e * F, F)

    counter = [0, 0]

    def sems(count):
        first = counter[0]
        counter[0] += count
        return first

    def send_sem():
        counter[1] += 1
        return counter[1] - 1

    def copy(src, dst, ks, k, dp, ex):
        return pltpu.make_async_remote_copy(
            src_ref=src,
            dst_ref=dst,
            send_sem=ss.at[ks],
            recv_sem=rs.at[k],
            device_id=(dp, ex),
            device_id_type=pl.DeviceIdType.MESH,
        )

    pending = []

    def sent(ref, ks):
        copy(ref, ref, ks, 0, me, sib).wait_send()

    def sent_later(ref, ks):
        pending.append(lambda: sent(ref, ks))

    def arrive(dst, k):
        copy(dst, dst, 0, k, me, sib).wait_recv()

    def rows16(ref, i):
        return ref.at[pl.ds(pl.multiple_of(i * CAP, CAP), CAP)]

    def one_row(ref, i):
        return ref.at[pl.ds(i, 1)]

    def some16(ref):
        return lambda i, count: ref.at[pl.ds(pl.multiple_of(i * CAP, CAP), count * CAP)]

    def some_rows(ref):
        return lambda i, count: ref.at[pl.ds(i, count)]

    class Spread:
        def __init__(self, src, dst, some, by_group=False):
            self.src, self.dst, self.some, self.by_group = src, dst, some, by_group
            self.ks = send_sem()
            self.base = sems(GROUPS if by_group else 1)
            sent_later(some(0, n_dp - 1), self.ks)

        def start_group(self, group, k):
            arrival = self.base + (my_group if self.by_group else 0)

            def step(kk, carry):
                t = group * z.gs + (me % z.gs + kk) % z.gs
                copy(self.src(t), self.dst(me), self.ks, arrival, t, e).start()
                return carry

            lax.fori_loop(1 if k == 0 else 0, z.gs, step, 0)

        def start(self):
            for k in range(GROUPS):
                self.start_group((my_group + k) % GROUPS, k)

        def wait_group(self, group, k):
            count = z.gs - 1 if k == 0 else z.gs
            if count:
                arrive(self.some(group * z.gs, count), self.base + group)

        def wait(self):
            arrive(self.some(0, n_dp - 1), self.base)

    class Gather:
        def __init__(self, ref, first, rows):
            self.ref, self.first, self.rows = ref, first, rows
            self.parts = ref.shape[1] // rows
            self.ks = send_sem()
            self.base = sems(4 * self.parts)
            sent_later(ref.at[pl.ds(0, 7)], self.ks)

        def part(self, block, q):
            return self.ref.at[block, pl.ds(pl.multiple_of(self.first(q), TILE), self.rows)]

        def go(self, q, t, block, peer):
            ref = self.part(block, q)
            copy(ref, ref, self.ks, self.base + 4 * q + t, me, peer).start()

        def start(self, q):
            self.go(q, 2, e, across)
            self.go(q, 0, e, right)
            self.go(q, 1, e, left)
            self.go(q, 3, e, sib)

        def mid(self, q):
            for t, block in ((0, left), (1, right), (2, across)):
                arrive(self.part(block, q), self.base + 4 * q + t)
                self.go(q, 3, block, sib)

        def end(self, q):
            four = self.ref.at[pl.ds(0, 4), pl.ds(pl.multiple_of(self.first(q), TILE), self.rows)]
            arrive(four, self.base + 4 * q + 3)

        def whole(self):
            for step in (self.start, self.mid, self.end):
                for q in range(self.parts):
                    step(q)

    class Exchange:
        def __init__(self, src, dst, ref):
            self.src, self.dst, self.ref = src, dst, ref
            self.ks = send_sem()
            self.base = sems(1)
            sent_later(ref.at[pl.ds(0, n_e - 1)], self.ks)

        def start(self, prepare=None):
            for p in (4, 5, 2, 3, 6, 7, 1):
                peer = 2 * ((x + p // 2) % 4) + (c + p % 2) % 2
                if prepare is not None:
                    prepare(peer)
                copy(self.src(peer), self.dst(e), self.ks, self.base, me, peer).start()

        def wait(self):
            arrive(self.ref.at[pl.ds(0, n_e - 1)], self.base)

    class Reduce:
        def __init__(self, first, n, partial, bufs):
            self.n, self.partial, self.first = n, partial, first
            self.sib_send, self.sib_recv, self.own, self.xs, self.landing = bufs
            self.ks = send_sem()
            self.base = sems(5)
            sent_later(x_all.at[pl.ds(0, 7), pl.ds(0, n)], self.ks)

        def piece(self):
            return pl.ds(pl.multiple_of(self.first, TILE), self.n)

        def local(self):
            for dx in (2, 1, 3, 0):
                block = 2 * ((x + dx) % 4) + (1 - c)
                mine = self.sib_send.at[dx, self.piece()]
                mine[...] = self.partial(block).astype(BF16)
                theirs = self.sib_recv.at[dx, self.piece()]
                copy(mine, theirs, self.ks, self.base + dx, me, sib).start()

        def pairs(self):
            for dx in (2, 1, 3, 0):
                there = 2 * ((x + dx) % 4) + c
                own = self.partial(there)
                theirs = self.sib_recv.at[dx, self.piece()]
                arrive(theirs, self.base + dx)
                both = own + theirs[...].astype(F32)
                if dx == 0:
                    self.own[self.piece(), :] = both
                else:
                    out = self.xs.at[dx - 1, self.piece()]
                    out[...] = both.astype(BF16)
                    to = self.landing.at[dx - 1, self.piece()]
                    copy(out, to, self.ks, self.base + 4, me, there).start()

        def total(self):
            arrive(self.landing.at[pl.ds(0, 3), self.piece()], self.base + 4)
            value = self.own[self.piece(), :]
            for i in range(3):
                value = value + self.landing[i, self.piece(), :].astype(F32)
            return value

    local = {}

    def load(name, src, dst):
        copy_in = pltpu.make_async_copy(src, dst, ls.at[len(local)])
        copy_in.start()
        local[name] = copy_in

    load("memory", memory_hbm, mem_all.at[e])
    load("grad", grad_hbm.at[:, pl.ds(col_e, F)], live)
    load("wo", wo_hbm, wo)
    load("tokens", tokens_hbm, tok)
    load("wq", wq_hbm, wq)
    load("wk", wk_hbm, wk)
    load("wv", wv_hbm, wv)
    load("wr", wr_hbm.at[:, pl.ds(col_e, F)], wr)
    load("down", down_hbm, down)
    load("up", up_hbm, up)

    barrier = pltpu.get_barrier_semaphore()

    def greet(kk, carry):
        pl.semaphore_signal(
            barrier, inc=1, device_id=((me + kk) % n_dp, e), device_id_type=pl.DeviceIdType.MESH
        )
        return carry

    lax.fori_loop(1, n_dp, greet, 0)
    for p in range(1, n_e):
        pl.semaphore_signal(
            barrier, inc=1, device_id=(me, (e + p) % n_e), device_id_type=pl.DeviceIdType.MESH
        )

    choice_rows = jnp.concatenate([routing_ref[s] for s in range(z.S)], axis=1)
    expert_row = iota((z.E, T), 0)
    hot_rows = [expert_row == choice_rows[i : i + 1] for i in range(2)]
    hot = [h.astype(F32) for h in hot_rows]
    before = (iota((T, T), 0) < iota((T, T), 1)).astype(BF16)
    counts = dot((hot[0] + hot[1]).astype(BF16), before)
    rank_rows = [jnp.sum(h * counts, axis=0, keepdims=True) for h in hot]
    slot_rows = [choice_rows[i : i + 1].astype(F32) * CAP + rank_rows[i] for i in range(2)]
    rank0, rank1, slot0, slot1 = to_columns(stack_rows(*rank_rows, *slot_rows), 4)
    rank, slot = [rank0, rank1], [slot0, slot1]
    slot_row = iota((R, T), 0)
    plan[...] = jnp.logical_or(slot_row == slot_rows[0].astype(jnp.int32), slot_row == slot_rows[1].astype(jnp.int32)).astype(BF16)
    slot_lane = iota((T, R), 1)
    plan0[...] = (slot_lane == slot[0].astype(jnp.int32)).astype(BF16)
    plan1[...] = (slot_lane == slot[1].astype(jnp.int32)).astype(BF16)

    lane_1 = iota((1, LANES), 1)
    note = jnp.zeros((1, LANES), jnp.int32)
    for k in range(z.S):
        note = jnp.where(lane_1 == k, src_ref[k], note)
        note = jnp.where(lane_1 == z.S + k, slen_ref[k], note)
    meta[pl.ds(me, 1), :] = note.astype(F32)

    local["grad"].wait()
    row_t = iota((T, 1), 0)
    length = jnp.zeros((T, 1), jnp.int32)
    for k in range(z.S):
        length = jnp.where((row_t >> log2(z.L)) == k, tlen_ref[k], length)
    alive = (row_t & (z.L - 1)) < length
    live[...] = jnp.where(alive, live[...].astype(F32), 0.0).astype(BF16)
    slots = dot(plan[...], live[...]).astype(BF16)
    g_send[...] = slots
    own_rows = pl.ds(pl.multiple_of(me * CAP, CAP), CAP)
    g_all[e, own_rows, :] = g_send[own_rows, :]

    pl.semaphore_wait(barrier, n_dp - 1 + n_e - 1)

    local["memory"].wait()
    memory_gather = Gather(mem_all, lambda q: q * (T // 2), T // 2)
    memory_gather.start(0)
    memory_gather.start(1)
    meta_spread = Spread(lambda t: one_row(meta, me), lambda i: one_row(meta, i), some_rows(meta))
    meta_spread.start()
    g_spread = Spread(
        lambda t: rows16(g_send, t), lambda i: rows16(g_all.at[e], i), some16(g_all.at[e])
    )
    g_spread.start()

    local["tokens"].wait()
    local["wq"].wait()
    rows_f = tok[...].astype(F32)
    centred = rows_f - jnp.mean(rows_f, axis=1, keepdims=True)
    variance = jnp.mean(centred * centred, axis=1, keepdims=True)
    normed = (centred * lax.rsqrt(variance + EPS) * again_ref[...]).astype(BF16)
    queries = dot(normed, wq[...]).astype(BF16)

    local["wo"].wait()
    for b in range(n_e):

        @pl.when(e == b)
        def _():
            ow_all[b] = wo[:, b * F : (b + 1) * F]

    ow_exchange = Exchange(
        lambda peer: wo.at[:, pl.ds(pl.multiple_of(peer * F, F), F)],
        lambda b: ow_all.at[b],
        ow_all,
    )
    for q in range(2):
        memory_gather.mid(q)
    for q in range(2):
        memory_gather.end(q)
    ow_exchange.start()

    local["wk"].wait()
    local["wv"].wait()
    keys = jnp.zeros((T, z.Hd), F32)
    values = jnp.zeros((T, z.Hd), F32)
    for b in range(n_e):
        block = mem_all[b]
        keys = keys + dot(block, wk[b * F : (b + 1) * F, :])
        values = values + dot(block, wv[b * F : (b + 1) * F, :])

    r_out = iota((2 * T, 2 * T), 0)
    r_in = iota((2 * T, 2 * T), 1)
    place = (
        ((r_out >> 3) & 1) * T + ((r_out >> 1) & 3) * z.L + ((r_out >> 4) << 1) + (r_out & 1)
    )
    order = (r_in == place).astype(BF16)

    middle_me = me % 2 == (me // 4 + c) % 2
    my_middle = me // 2

    def middle_dp(m):
        return 2 * m + (m // 2 + c) % 2

    class Relay:
        def __init__(self, send_buf, held, sorted_buf, recv_buf):
            self.send_buf, self.held, self.sorted_buf, self.recv_buf = (
                send_buf, held, sorted_buf, recv_buf,
            )
            self.out, self.back = sems(1), sems(1)
            self.ks_out, self.ks_back = send_sem(), send_sem()

        def each_middle(self, action):
            def step(kk, carry):
                m = (my_middle + kk) % z.mids

                @pl.when(middle_dp(m) != me)
                def _():
                    action(m)

                return carry

            lax.fori_loop(0, z.mids, step, 0)

        def first(self, m):
            copy(
                rows16(self.send_buf, m), rows16(self.held, me), self.ks_out, self.out,
                middle_dp(m), e,
            ).start()

        def start(self):
            self.each_middle(self.first)

            @pl.when(middle_me)
            def _():
                rows16(self.held, me)[...] = rows16(self.send_buf, my_middle)[...]

        def turn(self, transposed):
            @pl.when(middle_me)
            def _():
                arrive(some16(self.held)(0, n_dp - 1), self.out)
                self.sorted_buf[...] = dot(
                    relay_plan[...], self.held[...], 0 if transposed else 1, 0
                ).astype(BF16)

                def step(kk, carry):
                    j = (me + kk) % n_dp
                    copy(
                        rows16(self.sorted_buf, j), rows16(self.recv_buf, my_middle),
                        self.ks_back, self.back, j, e,
                    ).start()
                    return carry

                lax.fori_loop(1, n_dp, step, 0)
                rows16(self.recv_buf, my_middle)[...] = rows16(self.sorted_buf, me)[...]

        def end(self):
            @pl.when(middle_me)
            def _():
                arrive(some16(self.recv_buf)(0, z.mids - 1), self.back)

            @pl.when(jnp.logical_not(middle_me))
            def _():
                arrive(self.recv_buf, self.back)

        def finish(self):
            @pl.when(middle_me)
            def _():
                sent(some16(self.send_buf)(0, z.mids - 1), self.ks_out)
                sent(some16(self.sorted_buf)(0, n_dp - 1), self.ks_back)

            @pl.when(jnp.logical_not(middle_me))
            def _():
                sent(self.send_buf, self.ks_out)

    both = jnp.concatenate([keys.astype(BF16), values.astype(BF16)], axis=0)
    kv_send[...] = dot(order, both).astype(BF16)
    relay = Relay(kv_send, mid_buf, mid_out_buf, kv_recv)
    relay.start()

    meta_spread.wait()
    notes = meta[...]
    span = n_dp * TILE
    pick = ((iota((span, n_dp), 0) >> 4) == iota((span, n_dp), 1)).astype(BF16)
    spread_notes = dot(pick, notes.astype(BF16))
    wanted = ((iota((span, LANES), 0) >> 1) & 3) == iota((span, LANES), 1)
    source = jnp.sum(jnp.where(wanted, spread_notes, 0.0), axis=1, keepdims=True).astype(jnp.int32)
    p_row = iota((span, span), 0)
    p_col = iota((span, span), 1)
    relay_plan[...] = (p_col == (source * TILE + (p_row & (TILE - 1)))).astype(BF16)
    relay.turn(False)

    g_spread.wait()
    g_gather = Gather(g_all, lambda q: 0, R)
    g_gather.start(0)

    key_length = jnp.zeros((1, T), F32)
    key_at = iota((1, T), 1)
    n_row, n_lane = iota((n_dp, LANES), 0), iota((n_dp, LANES), 1)
    for k in range(z.S):
        here = jnp.logical_and(n_row == src_ref[k], n_lane == z.S + k)
        found = jnp.sum(jnp.where(here, notes, 0.0), axis=1, keepdims=True)
        found = jnp.sum(found, axis=0, keepdims=True)
        key_length = jnp.where((key_at >> log2(z.L)) == k, found, key_length)

    relay.end()
    kv = dot(order, kv_recv[...], 0, 0).astype(BF16)
    key_heads, value_heads = kv[:T], kv[T:]

    scaling = z.Hd ** (-0.5)
    same = (iota((T, T), 0) >> log2(z.L)) == (iota((T, T), 1) >> log2(z.L))
    inside = (key_at & (z.L - 1)).astype(F32) < key_length
    open_keys = jnp.logical_and(same, inside)
    scores = jnp.where(open_keys, dot(queries, key_heads, 1, 1) * scaling, -1e30)
    exps = jnp.exp(scores - jnp.max(scores, axis=1, keepdims=True))
    probabilities = exps / jnp.sum(exps, axis=1, keepdims=True)
    weights = probabilities.astype(BF16)
    att_all[e] = dot(weights, value_heads).astype(BF16)
    att_gather = Gather(att_all, lambda q: 0, T)
    att_gather.start(0)
    att_gather.mid(0)
    g_gather.mid(0)
    ow_exchange.wait()
    att_gather.end(0)

    heads_sum = jnp.zeros((T, F), F32)
    for b in range(n_e):
        heads_sum = heads_sum + dot(att_all[b], ow_all[b])
    hidden = (tok[:, pl.ds(col_e, F)].astype(F32) + heads_sum).astype(BF16).astype(F32)
    hid[...] = hidden
    part_sum = jnp.sum(hidden, axis=1, keepdims=True)
    off = hidden - part_sum * (1.0 / F)
    part_sq = jnp.sum(off * off, axis=1, keepdims=True)
    stat1[e] = to_rows([part_sum, part_sq])
    stat1_exchange = Exchange(lambda peer: stat1.at[e], lambda b: stat1.at[b], stat1)
    stat1_exchange.start()
    g_gather.end(0)
    stat1_exchange.wait()
    parts = [stat1[b] for b in range(n_e)]
    mean_row = sum(p[0:1] for p in parts) * (1.0 / D)
    square_row = sum(p[1:2] for p in parts)
    for p in parts:
        shift = p[0:1] * (1.0 / F) - mean_row
        square_row = square_row + F * (shift * shift)
    rstd_row = lax.rsqrt(square_row * (1.0 / D) + EPS)
    mean, rstd = to_columns(stack_rows(mean_row, rstd_row), 2)
    gain = fgain_ref[:, pl.ds(col_e, F)]
    unit = (hidden - mean) * rstd
    expert_in = (unit * gain).astype(BF16)
    unit_bf = unit.astype(BF16)

    x_send[...] = dot(plan[...], expert_in).astype(BF16)
    x_all[e, own_rows, :] = x_send[own_rows, :]
    x_spread = Spread(
        lambda t: rows16(x_send, t), lambda i: rows16(x_all.at[e], i), some16(x_all.at[e]), True
    )
    x_spread.start()
    local["wr"].wait()
    router = wr[...]
    lg_all[e] = dot(router, expert_in, 1, 1)
    lg_exchange = Exchange(lambda peer: lg_all.at[e], lambda b: lg_all.at[b], lg_all)
    lg_exchange.start()

    def unit_part(head):
        uw_send[head] = dot(unit_bf, ow_all[head], 1, 1)

    uw_exchange = Exchange(lambda peer: uw_send.at[peer], lambda b: uw_recv.at[b], uw_recv)
    uw_exchange.start(unit_part)
    uw_recv[e] = dot(unit_bf, ow_all[e], 1, 1)

    local["down"].wait()

    def down_back(q, carry):
        piece = pl.ds(pl.multiple_of(q * Q, Q), Q)
        total = jnp.zeros((Q, z.H), F32)
        for b in range(n_e):
            total = total + dot(g_all[b, piece, :], down[:, b * F : (b + 1) * F], 1, 1)
        u_buf[piece, :] = total
        return carry

    lax.fori_loop(0, 2, down_back, 0)

    lg_exchange.wait()
    logits = sum(lg_all[b] for b in range(n_e))
    chosen = [jnp.sum(jnp.where(h, logits, 0.0), axis=0, keepdims=True) for h in hot_rows]
    top = jnp.maximum(chosen[0], chosen[1])
    lifted = [jnp.exp(v - top) for v in chosen]
    share = [v / (lifted[0] + lifted[1]) for v in lifted]
    rank_lane = [
        (iota((T, LANES), 1) == rank[i].astype(jnp.int32)).astype(F32) for i in range(2)
    ]
    gate_rows = jnp.zeros((z.E, LANES), F32)
    for i in range(2):
        gate_rows = gate_rows + dot(jnp.where(hot_rows[i], share[i], 0.0), rank_lane[i], 1, 0, HI)
    gate_send[...] = gate_rows
    gate_recv[pl.ds(me, 1), :] = gate_send[pl.ds(me, 1), :]
    gate_spread = Spread(
        lambda t: one_row(gate_send, t), lambda i: one_row(gate_recv, i), some_rows(gate_recv)
    )
    gate_spread.start()
    lax.fori_loop(2, GROUPS, down_back, 0)

    def group_first(k):
        return ((my_group + GROUPS - k) % GROUPS) * Q

    x_gather = Gather(x_all, group_first, Q)
    local["up"].wait()
    reduces = []

    def expert_group(k):
        first = group_first(k)
        piece = pl.ds(pl.multiple_of(first, Q), Q)
        pre = jnp.zeros((Q, z.H), F32)
        for b in range(n_e):
            pre = pre + dot(x_all[b, piece, :], up[b * F : (b + 1) * F, :])
        cubic = pre * pre * pre
        slope_in = 0.7978845608028654 * (pre + 0.044715 * cubic)
        bend = jnp.tanh(slope_in)
        act = (pre * (0.5 * (1.0 + bend))).astype(BF16)
        act_buf[piece, :] = act
        slope = 0.5 * (1.0 + bend) + 0.5 * pre * (1.0 - bend * bend) * (
            0.7978845608028654 * (1.0 + 3.0 * 0.044715 * pre * pre)
        )
        grads = u_buf[piece, :]
        gates, pick, wanted = gate_column(first, Q)
        pg_buf[piece, :] = (gates * grads * slope).astype(BF16)
        dots = jnp.sum(act.astype(F32) * grads, axis=1, keepdims=True)
        return dot(pick, jnp.where(wanted, dots, 0.0), 0, 0, HI)

    def gate_column(first, rows):
        pick = (((iota((rows, n_dp), 0) + first) >> 4) == iota((rows, n_dp), 1)).astype(F32)
        wanted = (iota((rows, LANES), 0) & (CAP - 1)) == iota((rows, LANES), 1)
        spread_gates = dot(pick, gate_recv[...], 1, 0, HI)
        gates = jnp.sum(jnp.where(wanted, spread_gates, 0.0), axis=1, keepdims=True)
        return gates, pick, wanted

    def input_partial(first):
        def partial(block):
            piece = pl.ds(pl.multiple_of(first, Q), Q)
            rows = pl.ds(pl.multiple_of(block * F, F), F)
            return dot(pg_buf[piece, :], up[rows, :], 1, 1)

        return partial

    ret_spread = Spread(
        lambda t: rows16(ret_send, t), lambda i: rows16(ret_recv, i), some16(ret_recv)
    )
    bufs = (sib_send, sib_recv, own_sum, xs_send, xs_recv)

    def give_back(k):
        first = group_first(k)
        piece = pl.ds(pl.multiple_of(first, Q), Q)
        ret_send[piece, :] = reduces[k].total().astype(BF16)
        ret_spread.start_group((my_group + GROUPS - k) % GROUPS, k)

    gg_total = jnp.zeros((n_dp, LANES), F32)
    for step in range(GROUPS + 2):
        if step < GROUPS:
            x_spread.wait_group((my_group + GROUPS - step) % GROUPS, step)
            x_gather.start(step)
        if 1 <= step < GROUPS + 1:
            x_gather.mid(step - 1)
        if step == 2:
            gate_spread.wait()
        if step >= 2:
            k = step - 2
            x_gather.end(k)
            gg_total = gg_total + expert_group(k)
            reduces.append(Reduce(group_first(k), Q, input_partial(group_first(k)), bufs))
            reduces[k].local()
            reduces[k].pairs()

    gg_all[e] = gg_total
    gg_exchange = Exchange(lambda peer: gg_all.at[e], lambda b: gg_all.at[b], gg_all)
    gg_exchange.start()

    def up_back(b, carry):
        rows = pl.ds(pl.multiple_of(b * F, F), F)
        ug[rows, :] = dot(x_all[b], pg_buf[...], 0, 0).astype(BF16)
        return carry

    gates_all = gate_column(0, R)[0]

    def down_grad(b, carry):
        columns = pl.ds(pl.multiple_of(b * F, F), F)
        scaled = (g_all[b].astype(F32) * gates_all).astype(BF16)
        dg[:, columns] = dot(act_buf[...], scaled, 0, 0).astype(BF16)
        return carry

    give_back(0)
    gg_exchange.wait()
    gg_sum = sum(gg_all[b] for b in range(n_e))
    gg_send[...] = gg_sum
    gg_recv[pl.ds(me, 1), :] = gg_send[pl.ds(me, 1), :]
    gg_spread = Spread(
        lambda t: one_row(gg_send, t), lambda i: one_row(gg_recv, i), some_rows(gg_recv)
    )
    gg_spread.start()
    give_back(1)
    lax.fori_loop(0, n_e // 2, up_back, 0)
    give_back(2)
    lax.fori_loop(n_e // 2, n_e, up_back, 0)
    give_back(3)
    ret_recv[own_rows, :] = ret_send[own_rows, :]
    up_store = pltpu.make_async_copy(ug, up_out, ls.at[len(local)])
    up_store.start()
    lax.fori_loop(0, n_e // 2, down_grad, 0)

    gg_spread.wait()
    gate_grad = []
    for i in range(2):
        spread_gg = dot(gg_recv[...], rank_lane[i], 1, 1, HI)
        gate_grad.append(jnp.sum(jnp.where(hot_rows[i], spread_gg, 0.0), axis=0, keepdims=True))
    delta = share[0] * share[1] * (gate_grad[0] - gate_grad[1])
    logit_grad = jnp.where(hot_rows[0], delta, 0.0) - jnp.where(hot_rows[1], delta, 0.0)
    high = logit_grad.astype(BF16)
    low = (logit_grad - high.astype(F32)).astype(BF16)
    router_term = dot(high, router, 0, 0) + dot(low, router, 0, 0)
    share_columns = to_columns(stack_rows(share[0], share[1]), 2)

    ret_spread.wait()
    returned = ret_recv[...]
    ffn_in_grad = (
        share_columns[0] * dot(plan0[...], returned)
        + share_columns[1] * dot(plan1[...], returned)
        + router_term
    )

    scaled_in = ffn_in_grad * gain
    unit = (hid[...] - mean) * rstd
    stat2[e] = to_rows(
        [
            jnp.sum(scaled_in, axis=1, keepdims=True),
            jnp.sum(scaled_in * unit, axis=1, keepdims=True),
        ]
    )
    stat2_exchange = Exchange(lambda peer: stat2.at[e], lambda b: stat2.at[b], stat2)
    stat2_exchange.start()
    hg_all[e] = (live[...].astype(F32) + rstd * scaled_in).astype(BF16)
    hg_gather = Gather(hg_all, lambda q: q * (T // 2), T // 2)
    hg_gather.start(0)
    hg_gather.start(1)
    lax.fori_loop(n_e // 2, n_e, down_grad, 0)
    down_store = pltpu.make_async_copy(dg, down_out, ls.at[len(local) + 1])
    down_store.start()
    uw_exchange.wait()
    unit_heads = sum(uw_recv[b] for b in range(n_e))
    weight_sums = dot(jnp.ones((8, D), BF16), wo[...], 1, 1)[:1]
    hg_gather.mid(0)
    hg_gather.mid(1)
    stat2_exchange.wait()
    sums = sum(stat2[b] for b in range(n_e)) * (1.0 / D)
    mean_in, mean_unit = to_columns(sums, 2)
    hg_gather.end(0)
    hg_gather.end(1)

    att_grad = jnp.zeros((T, z.Hd), F32)
    for b in range(n_e):
        att_grad = att_grad + dot(hg_all[b], wo[:, b * F : (b + 1) * F], 1, 1)
    att_grad = att_grad - (rstd * mean_in) * weight_sums - (rstd * mean_unit) * unit_heads
    att_grad = att_grad.astype(BF16)
    value_grad = dot(weights, att_grad, 0, 0).astype(BF16)
    prob_grad = dot(att_grad, value_heads, 1, 1)
    inner = jnp.sum(probabilities * prob_grad, axis=1, keepdims=True)
    score_grad = (probabilities * (prob_grad - inner) * scaling).astype(BF16)
    key_grad = dot(score_grad, queries, 0, 0).astype(BF16)
    both = jnp.concatenate([key_grad, value_grad], axis=0)
    kvg_send[...] = dot(order, both).astype(BF16)
    relay_back = Relay(kvg_send, mid_buf2, mid_out2, kvg_recv)
    relay_back.start()
    relay_back.turn(True)
    relay_back.end()
    home = dot(order, kvg_recv[...], 0, 0).astype(BF16)
    home_keys, home_values = home[:T], home[T:]

    def memory_partial(block):
        rows = pl.ds(pl.multiple_of(block * F, F), F)
        return dot(home_keys, wk[rows, :], 1, 1) + dot(home_values, wv[rows, :], 1, 1)

    def memory_send(block):
        mg_send[block] = memory_partial(block).astype(BF16)

    memory_exchange = Exchange(lambda peer: mg_send.at[peer], lambda b: mg_recv.at[b], mg_recv)
    memory_exchange.start(memory_send)
    mg_recv[e] = jnp.zeros((T, F), BF16)
    own_part = memory_partial(e)
    memory_exchange.wait()
    mg[...] = (own_part + sum(mg_recv[b].astype(F32) for b in range(n_e))).astype(BF16)
    mem_store = pltpu.make_async_copy(mg, mem_out, ls.at[len(local) + 2])
    mem_store.start()

    relay.finish()
    relay_back.finish()
    for finish in pending:
        finish()
    up_store.wait()
    down_store.wait()
    mem_store.wait()
    assert counter[0] <= SEMS and counter[1] <= SENDS, counter


SEMS = 80
SENDS = 32


def hand_on(*refs):
    arrays, results, held = refs[0:3], refs[3:6], refs[6:9]
    in_sem, out_sem = refs[9:]
    pieces = []
    for a in range(3):
        rows = arrays[a].shape[0]
        cuts = 8 if rows >= 512 else 1
        for j in range(cuts):
            pieces.append((a, pl.ds(j * (rows // cuts), rows // cuts)))

    def step(source, target, i, sem):
        a, piece = pieces[i]
        return pltpu.make_async_copy(source[a].at[piece], target[a].at[piece], sem.at[i])

    for i in range(len(pieces)):
        step(arrays, held, i, in_sem).start()
    for i in range(len(pieces)):
        step(arrays, held, i, in_sem).wait()
        step(held, results, i, out_sem).start()
    for i in range(len(pieces)):
        step(held, results, i, out_sem).wait()


def build(mesh):
    n_dp, n_e = mesh.shape["dp"], mesh.shape["expert"]

    def body(
        tokens, memory, source_length, owner_device, source_device, target_length, routing,
        attn_gain, ffn_gain, query_weight, key_weight, value_weight, out_weight, router_weight,
        up_weight, down_weight, grad_out,
    ):
        sentences, length, width = tokens.shape
        z = Layout(
            n_dp, n_e, sentences, length, width, query_weight.shape[1], up_weight.shape[2],
            router_weight.shape[1],
        )
        T, D, F, R, H = z.T, z.D, z.F, z.R, z.H
        span = n_dp * TILE
        vm = pltpu.VMEM
        scratch = [
            vm((T, D), BF16), vm((T, F), BF16), vm((D, z.Hd), BF16), vm((D, z.Hd), BF16),
            vm((D, z.Hd), BF16), vm((z.Hd, D), BF16), vm((z.E, F), BF16), vm((D, H), BF16),
            vm((H, D), BF16),
            vm((n_e, T, F), BF16), vm((n_e, z.Hd, F), BF16), vm((n_e, T, z.Hd), BF16),
            vm((n_e, T, F), BF16), vm((n_e, R, F), BF16), vm((n_e, R, F), BF16),
            vm((R, F), BF16), vm((R, F), BF16), vm((R, F), BF16), vm((R, F), BF16),
            vm((n_dp, LANES), F32),
            vm((2 * T, z.Hd), BF16), vm((span, z.Hd), BF16), vm((span, z.Hd), BF16),
            vm((2 * T, z.Hd), BF16),
            vm((2 * T, z.Hd), BF16), vm((span, z.Hd), BF16), vm((span, z.Hd), BF16),
            vm((2 * T, z.Hd), BF16),
            vm((n_e, 8, T), F32), vm((n_e, 8, T), F32), vm((n_e, z.E, T), F32),
            vm((z.E, LANES), F32), vm((n_dp, LANES), F32), vm((n_e, n_dp, LANES), F32),
            vm((n_dp, LANES), F32), vm((n_dp, LANES), F32),
            vm((R, T), BF16), vm((T, R), BF16), vm((T, R), BF16), vm((span, span), BF16),
            vm((R, H), F32), vm((R, H), BF16), vm((R, H), BF16),
            vm((4, R, F), BF16), vm((4, R, F), BF16), vm((R, F), F32), vm((3, R, F), BF16),
            vm((3, R, F), BF16), vm((n_e, T, z.Hd), F32), vm((n_e, T, z.Hd), F32),
            vm((n_e, T, F), BF16), vm((n_e, T, F), BF16),
            vm((D, H), BF16), vm((H, D), BF16), vm((T, F), BF16), vm((T, F), F32),
            pltpu.SemaphoreType.DMA((SENDS,)), pltpu.SemaphoreType.DMA((SEMS,)),
            pltpu.SemaphoreType.DMA((16,)),
        ]
        smem = pl.BlockSpec(memory_space=pltpu.SMEM)
        vmem = pl.BlockSpec(memory_space=pltpu.VMEM)
        hbm = pl.BlockSpec(memory_space=pl.ANY)
        results = pl.pallas_call(
            functools.partial(layer_kernel, z),
            out_shape=(
                jax.ShapeDtypeStruct((T, F), BF16),
                jax.ShapeDtypeStruct((D, H), BF16),
                jax.ShapeDtypeStruct((H, D), BF16),
            ),
            in_specs=[smem] * 3 + [vmem] * 3 + [hbm] * 10,
            out_specs=(hbm, hbm, hbm),
            scratch_shapes=scratch,
            compiler_params=pltpu.CompilerParams(
                collective_id=0, has_side_effects=True, vmem_limit_bytes=56 * 1024 * 1024
            ),
            name="layer",
        )(
            source_device, source_length, target_length, jnp.transpose(routing, (0, 2, 1)),
            attn_gain[None], ffn_gain[None],
            tokens.reshape(T, D), memory.reshape(T, F), grad_out.reshape(T, D),
            query_weight, key_weight, value_weight, out_weight, router_weight.T,
            up_weight[0], down_weight[0],
        )
        mem_grad, up_grad, down_grad = pl.pallas_call(
            hand_on,
            out_shape=tuple(jax.ShapeDtypeStruct(r.shape, r.dtype) for r in results),
            in_specs=[hbm] * 3,
            out_specs=(hbm, hbm, hbm),
            scratch_shapes=[pltpu.VMEM(r.shape, r.dtype) for r in results]
            + [pltpu.SemaphoreType.DMA((17,)), pltpu.SemaphoreType.DMA((17,))],
            compiler_params=pltpu.CompilerParams(vmem_limit_bytes=56 * 1024 * 1024),
            name="hand_on",
        )(*results)
        return mem_grad.reshape(sentences, length, F), up_grad[None], down_grad[None]

    return body


def solution(mesh):
    in_specs = (
        P("dp", None, None),
        P("dp", None, "expert"),
        P("dp"),
        P("dp"),
        P("dp"),
        P("dp"),
        P("dp", None, None),
        P(),
        P(),
        P(None, "expert"),
        P(None, "expert"),
        P(None, "expert"),
        P("expert", None),
        P(),
        P("dp", None, "expert"),
        P("dp", "expert", None),
        P("dp", None, None),
    )
    out_specs = (P("dp", None, "expert"), P("dp", None, "expert"), P("dp", "expert", None))
    return jax.shard_map(
        build(mesh), mesh=mesh, in_specs=in_specs, out_specs=out_specs, check_vma=False
    )
```

```python
import functools

import jax
import jax.numpy as jnp
from jax import lax
from jax.experimental import pallas as pl
from jax.experimental.pallas import tpu as pltpu
from jax.sharding import PartitionSpec as P

F32 = jnp.float32
BF16 = jnp.bfloat16
HI = lax.Precision.HIGHEST
LANES = 128
CAP = 16
TILE = 16
GROUPS = 4
EPS = 1e-5


def dot(a, b, ca=1, cb=0, precision=None):
    return lax.dot_general(
        a, b, (((ca,), (cb,)), ((), ())), preferred_element_type=F32, precision=precision
    )


def iota(shape, dim):
    return lax.broadcasted_iota(jnp.int32, shape, dim)


def log2(value):
    return value.bit_length() - 1


def to_rows(columns):
    rows = columns[0].shape[0]
    lane = iota((rows, LANES), 1)
    packed = jnp.zeros((rows, LANES), F32)
    for i, column in enumerate(columns):
        packed = jnp.where(lane == i, column, packed)
    return packed.T[:8]


def to_columns(rows, count):
    padded = jnp.concatenate([rows, jnp.zeros((LANES - 8, rows.shape[1]), F32)], axis=0).T
    return [padded[:, i : i + 1] for i in range(count)]


def stack_rows(*rows):
    fill = jnp.zeros((8 - len(rows), rows[0].shape[1]), F32)
    return jnp.concatenate([*rows, fill], axis=0)


class Layout:
    def __init__(self, n_dp, n_e, sentences, length, width, head, hidden, experts):
        self.n_dp, self.n_e, self.n_x = n_dp, n_e, n_e // 2
        self.S, self.L, self.T = sentences, length, sentences * length
        self.D, self.F = width, width // n_e
        self.Hd, self.H, self.E = head, hidden, experts
        self.R = n_dp * CAP
        self.mids = n_dp // 2
        self.gs = n_dp // GROUPS
        self.Q = self.R // GROUPS


def layer_kernel(
    z,
    src_ref, slen_ref, tlen_ref, routing_ref, again_ref, fgain_ref,
    tokens_hbm, memory_hbm, grad_hbm, wq_hbm, wk_hbm, wv_hbm, wo_hbm, wr_hbm, up_hbm, down_hbm,
    mem_out, up_out, down_out,
    tok, live, wq, wk, wv, wo, wr, up, down,
    mem_all, ow_all, att_all, ag_send, ag_recv, x_all, g_all,
    g_send, x_send, ret_send, ret_recv,
    meta, kv_send, mid_buf, mid_out_buf, kv_recv, kvg_send, mid_buf2, mid_out2, kvg_recv,
    stat1, stat2, lg_all, gate_send, gate_recv, gg_all, gg_send, gg_recv,
    plan, plan0, plan1, relay_plan, u_buf, act_buf, pg_buf,
    sib_send, sib_recv, own_sum, held_sum, xs_send, far_recv, xs_recv, uw_send, uw_recv, mg_send, mg_recv,
    ug, dg, mg, hid,
    ss, rs, ls,
):
    n_dp, n_e, T, D, F, R, Q = z.n_dp, z.n_e, z.T, z.D, z.F, z.R, z.Q
    me = lax.axis_index("dp")
    e = lax.axis_index("expert")
    x, c = e // 2, e % 2
    xr, xl = (x + 1) % 4, (x + 3) % 4
    sib = 2 * x + (1 - c)
    right, left = 2 * xr + c, 2 * xl + c
    across = 2 * ((x + 2) % 4) + c
    my_group = me // z.gs
    col_e = pl.multiple_of(e * F, F)

    counter = [0, 0]

    def sems(count):
        first = counter[0]
        counter[0] += count
        return first

    def send_sem():
        counter[1] += 1
        return counter[1] - 1

    def copy(src, dst, ks, k, dp, ex):
        return pltpu.make_async_remote_copy(
            src_ref=src,
            dst_ref=dst,
            send_sem=ss.at[ks],
            recv_sem=rs.at[k],
            device_id=(dp, ex),
            device_id_type=pl.DeviceIdType.MESH,
        )

    pending = []

    def sent(ref, ks):
        copy(ref, ref, ks, 0, me, sib).wait_send()

    def sent_later(ref, ks):
        pending.append(lambda: sent(ref, ks))

    def arrive(dst, k):
        copy(dst, dst, 0, k, me, sib).wait_recv()

    def rows16(ref, i):
        return ref.at[pl.ds(pl.multiple_of(i * CAP, CAP), CAP)]

    def one_row(ref, i):
        return ref.at[pl.ds(i, 1)]

    def some16(ref):
        return lambda i, count: ref.at[pl.ds(pl.multiple_of(i * CAP, CAP), count * CAP)]

    def some_rows(ref):
        return lambda i, count: ref.at[pl.ds(i, count)]

    class Spread:
        def __init__(self, src, dst, some, by_group=False):
            self.src, self.dst, self.some, self.by_group = src, dst, some, by_group
            self.ks = send_sem()
            self.base = sems(GROUPS if by_group else 1)
            sent_later(some(0, n_dp - 1), self.ks)

        def start_group(self, group, k):
            arrival = self.base + (my_group if self.by_group else 0)

            def step(kk, carry):
                t = group * z.gs + (me % z.gs + kk) % z.gs
                copy(self.src(t), self.dst(me), self.ks, arrival, t, e).start()
                return carry

            lax.fori_loop(1 if k == 0 else 0, z.gs, step, 0)

        def start(self):
            for k in range(GROUPS):
                self.start_group((my_group + k) % GROUPS, k)

        def wait_group(self, group, k):
            count = z.gs - 1 if k == 0 else z.gs
            if count:
                arrive(self.some(group * z.gs, count), self.base + group)

        def wait(self):
            arrive(self.some(0, n_dp - 1), self.base)

    class Gather:
        def __init__(self, ref, first, rows, ringed=0):
            self.ref, self.first, self.rows, self.ringed = ref, first, rows, ringed
            self.parts = ref.shape[1] // rows
            self.ks = send_sem()
            self.base = sems(4 * self.parts)
            sent_later(ref.at[pl.ds(0, 7)], self.ks)

        def part(self, block, q):
            return self.ref.at[block, pl.ds(pl.multiple_of(self.first(q), TILE), self.rows)]

        def go(self, q, t, block, peer):
            ref = self.part(block, q)
            copy(ref, ref, self.ks, self.base + 4 * q + t, me, peer).start()

        def start(self, q):
            if q >= self.ringed:
                self.go(q, 2, e, across)
            self.go(q, 0, e, right)
            self.go(q, 1, e, left)
            self.go(q, 3, e, sib)

        def mid(self, q):
            for t, block, onward in ((0, left, right), (1, right, left)):
                arrive(self.part(block, q), self.base + 4 * q + t)
                if q < self.ringed and t == q % 2:
                    self.go(q, 2, block, onward)
                self.go(q, 3, block, sib)
            if q >= self.ringed:
                self.far(q)

        def far(self, q):
            arrive(self.part(across, q), self.base + 4 * q + 2)
            self.go(q, 3, across, sib)

        def end(self, q):
            four = self.ref.at[pl.ds(0, 4), pl.ds(pl.multiple_of(self.first(q), TILE), self.rows)]
            arrive(four, self.base + 4 * q + 3)

        def whole(self):
            for step in (self.start, self.mid, self.end):
                for q in range(self.parts):
                    step(q)

    class Exchange:
        def __init__(self, src, dst, ref):
            self.src, self.dst, self.ref = src, dst, ref
            self.ks = send_sem()
            self.base = sems(1)
            sent_later(ref.at[pl.ds(0, n_e - 1)], self.ks)

        def start(self, prepare=None):
            for p in (4, 5, 2, 3, 6, 7, 1):
                peer = 2 * ((x + p // 2) % 4) + (c + p % 2) % 2
                if prepare is not None:
                    prepare(peer)
                copy(self.src(peer), self.dst(e), self.ks, self.base, me, peer).start()

        def wait(self):
            arrive(self.ref.at[pl.ds(0, n_e - 1)], self.base)

    class Reduce:
        def __init__(self, first, n, partial, bufs, ring=None):
            self.n, self.partial, self.first, self.ring = n, partial, first, ring
            self.sib_send, self.sib_recv, self.own, self.held, self.xs, self.far, self.landing = bufs
            self.ks = send_sem()
            self.base = sems(6)
            sent_later(x_all.at[pl.ds(0, 7), pl.ds(0, n)], self.ks)

        def piece(self):
            return pl.ds(pl.multiple_of(self.first, TILE), self.n)

        def local(self):
            for dx in (2, 1, 3, 0):
                block = 2 * ((x + dx) % 4) + (1 - c)
                mine = self.sib_send.at[dx, self.piece()]
                mine[...] = self.partial(block).astype(BF16)
                theirs = self.sib_recv.at[dx, self.piece()]
                copy(mine, theirs, self.ks, self.base + dx, me, sib).start()

        def put(self, dx, value, landing, there, t):
            out = self.xs.at[dx - 1, self.piece()]
            out[...] = value.astype(BF16)
            copy(out, landing, self.ks, self.base + t, me, there).start()

        def pairs(self):
            waits = {None: None, 0: 1, 1: 3}[self.ring]
            for dx in (2, 1, 3, 0):
                there = 2 * ((x + dx) % 4) + c
                own = self.partial(there)
                theirs = self.sib_recv.at[dx, self.piece()]
                arrive(theirs, self.base + dx)
                both = own + theirs[...].astype(F32)
                if dx == 0:
                    self.own[self.piece(), :] = both
                elif dx == waits:
                    self.held[self.piece(), :] = both
                elif dx == 2 and self.ring is not None:
                    by = left if self.ring else right
                    self.put(dx, both, self.far.at[self.piece()], by, 5)
                else:
                    self.put(dx, both, self.landing.at[dx - 1, self.piece()], there, 4)

        def onward(self):
            dx, there = (3, left) if self.ring else (1, right)
            arrive(self.far.at[self.piece()], self.base + 5)
            both = self.held[self.piece(), :] + self.far[self.piece(), :].astype(F32)
            self.put(dx, both, self.landing.at[dx - 1, self.piece()], there, 4)

        def total(self):
            parts = (0, 1, 2) if self.ring is None else (0, 2)
            arrive(self.landing.at[pl.ds(0, len(parts)), self.piece()], self.base + 4)
            value = self.own[self.piece(), :]
            for i in parts:
                value = value + self.landing[i, self.piece(), :].astype(F32)
            return value

    def group(k):
        return (my_group + GROUPS - k) % GROUPS

    def group_first(k):
        return group(k) * Q

    local = {}

    def load(name, src, dst):
        copy_in = pltpu.make_async_copy(src, dst, ls.at[len(local)])
        copy_in.start()
        local[name] = copy_in

    load("memory", memory_hbm, mem_all.at[e])
    load("grad", grad_hbm.at[:, pl.ds(col_e, F)], live)
    load("wo", wo_hbm, wo)
    load("tokens", tokens_hbm, tok)
    load("wq", wq_hbm, wq)
    load("wk", wk_hbm, wk)
    load("wv", wv_hbm, wv)
    load("wr", wr_hbm.at[:, pl.ds(col_e, F)], wr)
    load("down", down_hbm, down)
    load("up", up_hbm, up)

    barrier = pltpu.get_barrier_semaphore()

    def greet(kk, carry):
        pl.semaphore_signal(
            barrier, inc=1, device_id=((me + kk) % n_dp, e), device_id_type=pl.DeviceIdType.MESH
        )
        return carry

    lax.fori_loop(1, n_dp, greet, 0)
    for p in range(1, n_e):
        pl.semaphore_signal(
            barrier, inc=1, device_id=(me, (e + p) % n_e), device_id_type=pl.DeviceIdType.MESH
        )

    choice_rows = jnp.concatenate([routing_ref[s] for s in range(z.S)], axis=1)
    expert_row = iota((z.E, T), 0)
    hot_rows = [expert_row == choice_rows[i : i + 1] for i in range(2)]
    hot = [h.astype(F32) for h in hot_rows]
    before = (iota((T, T), 0) < iota((T, T), 1)).astype(BF16)
    counts = dot((hot[0] + hot[1]).astype(BF16), before)
    rank_rows = [jnp.sum(h * counts, axis=0, keepdims=True) for h in hot]
    slot_rows = [choice_rows[i : i + 1].astype(F32) * CAP + rank_rows[i] for i in range(2)]
    rank0, rank1, slot0, slot1 = to_columns(stack_rows(*rank_rows, *slot_rows), 4)
    rank, slot = [rank0, rank1], [slot0, slot1]
    slot_row = iota((R, T), 0)
    plan[...] = jnp.logical_or(slot_row == slot_rows[0].astype(jnp.int32), slot_row == slot_rows[1].astype(jnp.int32)).astype(BF16)
    slot_lane = iota((T, R), 1)
    plan0[...] = (slot_lane == slot[0].astype(jnp.int32)).astype(BF16)
    plan1[...] = (slot_lane == slot[1].astype(jnp.int32)).astype(BF16)

    lane_1 = iota((1, LANES), 1)
    note = jnp.zeros((1, LANES), jnp.int32)
    for k in range(z.S):
        note = jnp.where(lane_1 == k, src_ref[k], note)
        note = jnp.where(lane_1 == z.S + k, slen_ref[k], note)
    meta[pl.ds(me, 1), :] = note.astype(F32)

    local["grad"].wait()
    row_t = iota((T, 1), 0)
    length = jnp.zeros((T, 1), jnp.int32)
    for k in range(z.S):
        length = jnp.where((row_t >> log2(z.L)) == k, tlen_ref[k], length)
    alive = (row_t & (z.L - 1)) < length
    live[...] = jnp.where(alive, live[...].astype(F32), 0.0).astype(BF16)
    slots = dot(plan[...], live[...]).astype(BF16)
    g_send[...] = slots
    own_rows = pl.ds(pl.multiple_of(me * CAP, CAP), CAP)
    g_all[e, own_rows, :] = g_send[own_rows, :]

    pl.semaphore_wait(barrier, n_dp - 1 + n_e - 1)

    local["memory"].wait()
    memory_gather = Gather(mem_all, lambda q: q * (T // 2), T // 2)
    memory_gather.start(0)
    memory_gather.start(1)
    meta_spread = Spread(lambda t: one_row(meta, me), lambda i: one_row(meta, i), some_rows(meta))
    meta_spread.start()
    g_spread = Spread(
        lambda t: rows16(g_send, t), lambda i: rows16(g_all.at[e], i), some16(g_all.at[e]), True
    )
    g_gather = Gather(g_all, group_first, Q)
    for k in range(2):
        g_spread.start_group((my_group + k) % GROUPS, k)

    local["tokens"].wait()
    local["wq"].wait()
    rows_f = tok[...].astype(F32)
    centred = rows_f - jnp.mean(rows_f, axis=1, keepdims=True)
    variance = jnp.mean(centred * centred, axis=1, keepdims=True)
    normed = (centred * lax.rsqrt(variance + EPS) * again_ref[...]).astype(BF16)
    queries = dot(normed, wq[...]).astype(BF16)

    local["wo"].wait()
    for b in range(n_e):

        @pl.when(e == b)
        def _():
            ow_all[b] = wo[:, b * F : (b + 1) * F]

    ow_exchange = Exchange(
        lambda peer: wo.at[:, pl.ds(pl.multiple_of(peer * F, F), F)],
        lambda b: ow_all.at[b],
        ow_all,
    )
    for q in range(2):
        memory_gather.mid(q)
    for q in range(2):
        memory_gather.end(q)
    ow_exchange.start()

    local["wk"].wait()
    local["wv"].wait()
    keys = jnp.zeros((T, z.Hd), F32)
    values = jnp.zeros((T, z.Hd), F32)
    for b in range(n_e):
        block = mem_all[b]
        keys = keys + dot(block, wk[b * F : (b + 1) * F, :])
        values = values + dot(block, wv[b * F : (b + 1) * F, :])

    r_out = iota((2 * T, 2 * T), 0)
    r_in = iota((2 * T, 2 * T), 1)
    place = (
        ((r_out >> 3) & 1) * T + ((r_out >> 1) & 3) * z.L + ((r_out >> 4) << 1) + (r_out & 1)
    )
    order = (r_in == place).astype(BF16)

    middle_me = me % 2 == (me // 4 + c) % 2
    my_middle = me // 2

    def middle_dp(m):
        return 2 * m + (m // 2 + c) % 2

    class Relay:
        def __init__(self, send_buf, held, sorted_buf, recv_buf):
            self.send_buf, self.held, self.sorted_buf, self.recv_buf = (
                send_buf, held, sorted_buf, recv_buf,
            )
            self.out, self.back = sems(1), sems(1)
            self.ks_out, self.ks_back = send_sem(), send_sem()

        def each_middle(self, action):
            def step(kk, carry):
                m = (my_middle + kk) % z.mids

                @pl.when(middle_dp(m) != me)
                def _():
                    action(m)

                return carry

            lax.fori_loop(0, z.mids, step, 0)

        def first(self, m):
            copy(
                rows16(self.send_buf, m), rows16(self.held, me), self.ks_out, self.out,
                middle_dp(m), e,
            ).start()

        def start(self):
            self.each_middle(self.first)

            @pl.when(middle_me)
            def _():
                rows16(self.held, me)[...] = rows16(self.send_buf, my_middle)[...]

        def turn(self, transposed):
            @pl.when(middle_me)
            def _():
                arrive(some16(self.held)(0, n_dp - 1), self.out)
                self.sorted_buf[...] = dot(
                    relay_plan[...], self.held[...], 0 if transposed else 1, 0
                ).astype(BF16)

                def step(kk, carry):
                    j = (me + kk) % n_dp
                    copy(
                        rows16(self.sorted_buf, j), rows16(self.recv_buf, my_middle),
                        self.ks_back, self.back, j, e,
                    ).start()
                    return carry

                lax.fori_loop(1, n_dp, step, 0)
                rows16(self.recv_buf, my_middle)[...] = rows16(self.sorted_buf, me)[...]

        def end(self):
            @pl.when(middle_me)
            def _():
                arrive(some16(self.recv_buf)(0, z.mids - 1), self.back)

            @pl.when(jnp.logical_not(middle_me))
            def _():
                arrive(self.recv_buf, self.back)

        def finish(self):
            @pl.when(middle_me)
            def _():
                sent(some16(self.send_buf)(0, z.mids - 1), self.ks_out)
                sent(some16(self.sorted_buf)(0, n_dp - 1), self.ks_back)

            @pl.when(jnp.logical_not(middle_me))
            def _():
                sent(self.send_buf, self.ks_out)

    both = jnp.concatenate([keys.astype(BF16), values.astype(BF16)], axis=0)
    kv_send[...] = dot(order, both).astype(BF16)
    relay = Relay(kv_send, mid_buf, mid_out_buf, kv_recv)
    relay.start()

    meta_spread.wait()
    notes = meta[...]
    span = n_dp * TILE
    pick = ((iota((span, n_dp), 0) >> 4) == iota((span, n_dp), 1)).astype(BF16)
    spread_notes = dot(pick, notes.astype(BF16))
    wanted = ((iota((span, LANES), 0) >> 1) & 3) == iota((span, LANES), 1)
    source = jnp.sum(jnp.where(wanted, spread_notes, 0.0), axis=1, keepdims=True).astype(jnp.int32)
    p_row = iota((span, span), 0)
    p_col = iota((span, span), 1)
    relay_plan[...] = (p_col == (source * TILE + (p_row & (TILE - 1)))).astype(BF16)
    for k in range(2):
        g_spread.wait_group(group(k), k)
        g_gather.start(k)
    relay.turn(False)
    for k in range(2, GROUPS):
        g_spread.start_group((my_group + k) % GROUPS, k)
    g_gather.mid(0)

    key_length = jnp.zeros((1, T), F32)
    key_at = iota((1, T), 1)
    n_row, n_lane = iota((n_dp, LANES), 0), iota((n_dp, LANES), 1)
    for k in range(z.S):
        here = jnp.logical_and(n_row == src_ref[k], n_lane == z.S + k)
        found = jnp.sum(jnp.where(here, notes, 0.0), axis=1, keepdims=True)
        found = jnp.sum(found, axis=0, keepdims=True)
        key_length = jnp.where((key_at >> log2(z.L)) == k, found, key_length)

    relay.end()
    kv = dot(order, kv_recv[...], 0, 0).astype(BF16)
    key_heads, value_heads = kv[:T], kv[T:]

    scaling = z.Hd ** (-0.5)
    same = (iota((T, T), 0) >> log2(z.L)) == (iota((T, T), 1) >> log2(z.L))
    inside = (key_at & (z.L - 1)).astype(F32) < key_length
    open_keys = jnp.logical_and(same, inside)
    scores = jnp.where(open_keys, dot(queries, key_heads, 1, 1) * scaling, -1e30)
    exps = jnp.exp(scores - jnp.max(scores, axis=1, keepdims=True))
    probabilities = exps / jnp.sum(exps, axis=1, keepdims=True)
    weights = probabilities.astype(BF16)
    att_all[e] = dot(weights, value_heads).astype(BF16)
    att_gather = Gather(att_all, lambda q: 0, T)
    att_gather.start(0)
    g_gather.mid(1)
    g_spread.wait_group(group(2), 2)
    g_gather.start(2)
    att_gather.mid(0)
    ow_exchange.wait()
    att_gather.end(0)

    heads_sum = jnp.zeros((T, F), F32)
    for b in range(n_e):
        heads_sum = heads_sum + dot(att_all[b], ow_all[b])
    hidden = (tok[:, pl.ds(col_e, F)].astype(F32) + heads_sum).astype(BF16).astype(F32)
    hid[...] = hidden
    part_sum = jnp.sum(hidden, axis=1, keepdims=True)
    off = hidden - part_sum * (1.0 / F)
    part_sq = jnp.sum(off * off, axis=1, keepdims=True)
    stat1[e] = to_rows([part_sum, part_sq])
    stat1_exchange = Exchange(lambda peer: stat1.at[e], lambda b: stat1.at[b], stat1)
    stat1_exchange.start()
    g_gather.mid(2)
    stat1_exchange.wait()
    g_spread.wait_group(group(3), 3)
    g_gather.start(3)
    parts = [stat1[b] for b in range(n_e)]
    mean_row = sum(p[0:1] for p in parts) * (1.0 / D)
    square_row = sum(p[1:2] for p in parts)
    for p in parts:
        shift = p[0:1] * (1.0 / F) - mean_row
        square_row = square_row + F * (shift * shift)
    rstd_row = lax.rsqrt(square_row * (1.0 / D) + EPS)
    mean, rstd = to_columns(stack_rows(mean_row, rstd_row), 2)
    gain = fgain_ref[:, pl.ds(col_e, F)]
    unit = (hidden - mean) * rstd
    expert_in = (unit * gain).astype(BF16)

    x_send[...] = dot(plan[...], expert_in).astype(BF16)
    x_all[e, own_rows, :] = x_send[own_rows, :]
    x_spread = Spread(
        lambda t: rows16(x_send, t), lambda i: rows16(x_all.at[e], i), some16(x_all.at[e]), True
    )
    x_spread.start()
    local["wr"].wait()
    router = wr[...]
    lg_all[e] = dot(router, expert_in, 1, 1)
    lg_exchange = Exchange(lambda peer: lg_all.at[e], lambda b: lg_all.at[b], lg_all)
    lg_exchange.start()

    local["down"].wait()

    def down_back(k):
        piece = pl.ds(pl.multiple_of(group_first(k), Q), Q)
        total = jnp.zeros((Q, z.H), F32)
        for b in range(n_e):
            total = total + dot(g_all[b, piece, :], down[:, b * F : (b + 1) * F], 1, 1)
        u_buf[piece, :] = total

    x_gather = Gather(x_all, group_first, Q, 2)

    def x_start(k):
        x_spread.wait_group(group(k), k)
        x_gather.start(k)

    g_gather.end(0)
    down_back(0)
    x_start(0)
    g_gather.end(1)
    down_back(1)
    x_start(1)

    lg_exchange.wait()
    logits = sum(lg_all[b] for b in range(n_e))
    chosen = [jnp.sum(jnp.where(h, logits, 0.0), axis=0, keepdims=True) for h in hot_rows]
    top = jnp.maximum(chosen[0], chosen[1])
    lifted = [jnp.exp(v - top) for v in chosen]
    share = [v / (lifted[0] + lifted[1]) for v in lifted]
    rank_lane = [
        (iota((T, LANES), 1) == rank[i].astype(jnp.int32)).astype(F32) for i in range(2)
    ]
    gate_rows = jnp.zeros((z.E, LANES), F32)
    for i in range(2):
        gate_rows = gate_rows + dot(jnp.where(hot_rows[i], share[i], 0.0), rank_lane[i], 1, 0, HI)
    gate_send[...] = gate_rows
    gate_recv[pl.ds(me, 1), :] = gate_send[pl.ds(me, 1), :]
    gate_spread = Spread(
        lambda t: one_row(gate_send, t), lambda i: one_row(gate_recv, i), some_rows(gate_recv)
    )
    gate_spread.start()
    g_gather.mid(3)
    g_gather.end(2)
    down_back(2)
    x_start(2)
    g_gather.end(3)
    down_back(3)
    x_start(3)

    local["up"].wait()
    reduces = []

    def expert_group(k):
        first = group_first(k)
        piece = pl.ds(pl.multiple_of(first, Q), Q)
        pre = jnp.zeros((Q, z.H), F32)
        for b in range(n_e):
            pre = pre + dot(x_all[b, piece, :], up[b * F : (b + 1) * F, :])
        cubic = pre * pre * pre
        slope_in = 0.7978845608028654 * (pre + 0.044715 * cubic)
        bend = jnp.tanh(slope_in)
        act = (pre * (0.5 * (1.0 + bend))).astype(BF16)
        act_buf[piece, :] = act
        slope = 0.5 * (1.0 + bend) + 0.5 * pre * (1.0 - bend * bend) * (
            0.7978845608028654 * (1.0 + 3.0 * 0.044715 * pre * pre)
        )
        grads = u_buf[piece, :]
        steep = grads * slope
        u_buf[piece, :] = steep
        pg_buf[piece, :] = steep.astype(BF16)
        pick, wanted = slot_masks(first, Q)
        dots = jnp.sum(act.astype(F32) * grads, axis=1, keepdims=True)
        return dot(pick, jnp.where(wanted, dots, 0.0), 0, 0, HI)

    def slot_masks(first, rows):
        pick = (((iota((rows, n_dp), 0) + first) >> 4) == iota((rows, n_dp), 1)).astype(F32)
        wanted = (iota((rows, LANES), 0) & (CAP - 1)) == iota((rows, LANES), 1)
        return pick, wanted

    def input_partial(first):
        def partial(block):
            piece = pl.ds(pl.multiple_of(first, Q), Q)
            rows = pl.ds(pl.multiple_of(block * F, F), F)
            return dot(pg_buf[piece, :], up[rows, :], 1, 1)

        return partial

    ret_spread = Spread(
        lambda t: rows16(ret_send, t), lambda i: rows16(ret_recv, i), some16(ret_recv)
    )
    bufs = (sib_send, sib_recv, own_sum, held_sum, xs_send, far_recv, xs_recv)

    def give_back(k):
        first = group_first(k)
        piece = pl.ds(pl.multiple_of(first, Q), Q)
        ret_send[piece, :] = reduces[k].total().astype(BF16)
        ret_spread.start_group(group(k), k)

    gg_total = jnp.zeros((n_dp, LANES), F32)
    x_gather.mid(0)
    x_gather.mid(1)
    x_gather.far(0)
    for k in range(GROUPS):
        if k + 2 < GROUPS:
            x_gather.mid(k + 2)
        if k == 0:
            x_gather.far(1)
        x_gather.end(k)
        gg_total = gg_total + expert_group(k)
        if k == GROUPS - 1:
            gg_all[e] = gg_total
            gg_exchange = Exchange(lambda peer: gg_all.at[e], lambda b: gg_all.at[b], gg_all)
            gg_exchange.start()
        reduces.append(
            Reduce(group_first(k), Q, input_partial(group_first(k)), bufs, k if k < 2 else None)
        )
        reduces[k].local()
        reduces[k].pairs()
        if k in (1, 2):
            reduces[k - 1].onward()

    def up_back(b, carry):
        rows = pl.ds(pl.multiple_of(b * F, F), F)
        ug[rows, :] = dot(x_all[b], pg_buf[...], 0, 0).astype(BF16)
        return carry

    pick, wanted = slot_masks(0, R)
    gate_spread.wait()
    spread_gates = dot(pick, gate_recv[...], 1, 0, HI)
    gates_all = jnp.sum(jnp.where(wanted, spread_gates, 0.0), axis=1, keepdims=True)

    def down_grad(b, carry):
        columns = pl.ds(pl.multiple_of(b * F, F), F)
        scaled = (g_all[b].astype(F32) * gates_all).astype(BF16)
        dg[:, columns] = dot(act_buf[...], scaled, 0, 0).astype(BF16)
        return carry

    give_back(0)
    gg_exchange.wait()
    gg_sum = sum(gg_all[b] for b in range(n_e))
    gg_send[...] = gg_sum
    gg_recv[pl.ds(me, 1), :] = gg_send[pl.ds(me, 1), :]
    gg_spread = Spread(
        lambda t: one_row(gg_send, t), lambda i: one_row(gg_recv, i), some_rows(gg_recv)
    )
    gg_spread.start()
    give_back(1)
    pg_buf[...] = (gates_all * u_buf[...]).astype(BF16)
    lax.fori_loop(0, n_e // 2, up_back, 0)
    give_back(2)
    lax.fori_loop(n_e // 2, n_e, up_back, 0)
    give_back(3)
    ret_recv[own_rows, :] = ret_send[own_rows, :]

    unit_bf = ((hid[...] - mean) * rstd).astype(BF16)

    def unit_part(head):
        uw_send[head] = dot(unit_bf, ow_all[head], 1, 1).astype(BF16)

    uw_exchange = Exchange(lambda peer: uw_send.at[peer], lambda b: uw_recv.at[b], uw_recv)
    uw_exchange.start(unit_part)
    uw_recv[e] = dot(unit_bf, ow_all[e], 1, 1).astype(BF16)

    up_store = pltpu.make_async_copy(ug, up_out, ls.at[len(local)])
    up_store.start()
    lax.fori_loop(0, n_e // 2, down_grad, 0)

    gg_spread.wait()
    gate_grad = []
    for i in range(2):
        spread_gg = dot(gg_recv[...], rank_lane[i], 1, 1, HI)
        gate_grad.append(jnp.sum(jnp.where(hot_rows[i], spread_gg, 0.0), axis=0, keepdims=True))
    delta = share[0] * share[1] * (gate_grad[0] - gate_grad[1])
    logit_grad = jnp.where(hot_rows[0], delta, 0.0) - jnp.where(hot_rows[1], delta, 0.0)
    high = logit_grad.astype(BF16)
    low = (logit_grad - high.astype(F32)).astype(BF16)
    router_term = dot(high, router, 0, 0) + dot(low, router, 0, 0)
    share_columns = to_columns(stack_rows(share[0], share[1]), 2)

    ret_spread.wait()
    returned = ret_recv[...]
    ffn_in_grad = (
        (share_columns[0] * share_columns[0]) * dot(plan0[...], returned)
        + (share_columns[1] * share_columns[1]) * dot(plan1[...], returned)
        + router_term
    )

    scaled_in = ffn_in_grad * gain
    unit = (hid[...] - mean) * rstd
    stat2[e] = to_rows(
        [
            jnp.sum(scaled_in, axis=1, keepdims=True),
            jnp.sum(scaled_in * unit, axis=1, keepdims=True),
        ]
    )
    stat2_exchange = Exchange(lambda peer: stat2.at[e], lambda b: stat2.at[b], stat2)
    stat2_exchange.start()
    sent_grad = (live[...].astype(F32) + rstd * scaled_in).astype(BF16)

    def head_part(head):
        ag_send[head] = dot(sent_grad, ow_all[head], 1, 1).astype(BF16)

    ag_exchange = Exchange(lambda peer: ag_send.at[peer], lambda b: ag_recv.at[b], ag_recv)
    ag_exchange.start(head_part)
    ag_recv[e] = jnp.zeros((T, z.Hd), BF16)
    att_grad = dot(sent_grad, ow_all[e], 1, 1)
    lax.fori_loop(n_e // 2, n_e, down_grad, 0)
    down_store = pltpu.make_async_copy(dg, down_out, ls.at[len(local) + 1])
    down_store.start()
    uw_exchange.wait()
    unit_heads = sum(uw_recv[b].astype(F32) for b in range(n_e))
    weight_sums = dot(jnp.ones((8, D), BF16), wo[...], 1, 1)[:1]
    stat2_exchange.wait()
    sums = sum(stat2[b] for b in range(n_e)) * (1.0 / D)
    mean_in, mean_unit = to_columns(sums, 2)
    ag_exchange.wait()

    att_grad = att_grad + sum(ag_recv[b].astype(F32) for b in range(n_e))
    att_grad = att_grad - (rstd * mean_in) * weight_sums - (rstd * mean_unit) * unit_heads
    att_grad = att_grad.astype(BF16)
    value_grad = dot(weights, att_grad, 0, 0).astype(BF16)
    prob_grad = dot(att_grad, value_heads, 1, 1)
    inner = jnp.sum(probabilities * prob_grad, axis=1, keepdims=True)
    score_grad = (probabilities * (prob_grad - inner) * scaling).astype(BF16)
    key_grad = dot(score_grad, queries, 0, 0).astype(BF16)
    both = jnp.concatenate([key_grad, value_grad], axis=0)
    kvg_send[...] = dot(order, both).astype(BF16)
    relay_back = Relay(kvg_send, mid_buf2, mid_out2, kvg_recv)
    relay_back.start()
    relay_back.turn(True)
    relay_back.end()
    home = dot(order, kvg_recv[...], 0, 0).astype(BF16)
    home_keys, home_values = home[:T], home[T:]

    def memory_partial(block):
        rows = pl.ds(pl.multiple_of(block * F, F), F)
        return dot(home_keys, wk[rows, :], 1, 1) + dot(home_values, wv[rows, :], 1, 1)

    def memory_send(block):
        mg_send[block] = memory_partial(block).astype(BF16)

    memory_exchange = Exchange(lambda peer: mg_send.at[peer], lambda b: mg_recv.at[b], mg_recv)
    memory_exchange.start(memory_send)
    mg_recv[e] = jnp.zeros((T, F), BF16)
    own_part = memory_partial(e)
    memory_exchange.wait()
    mg[...] = (own_part + sum(mg_recv[b].astype(F32) for b in range(n_e))).astype(BF16)
    mem_store = pltpu.make_async_copy(mg, mem_out, ls.at[len(local) + 2])
    mem_store.start()

    relay.finish()
    relay_back.finish()
    for finish in pending:
        finish()
    up_store.wait()
    down_store.wait()
    mem_store.wait()
    assert counter[0] <= SEMS and counter[1] <= SENDS, counter


SEMS = 96
SENDS = 32


def hand_on(*refs):
    arrays, results, held = refs[0:3], refs[3:6], refs[6:9]
    in_sem, out_sem = refs[9:]
    pieces = []
    for a in range(3):
        rows = arrays[a].shape[0]
        cuts = 8 if rows >= 512 else 1
        for j in range(cuts):
            pieces.append((a, pl.ds(j * (rows // cuts), rows // cuts)))

    def step(source, target, i, sem):
        a, piece = pieces[i]
        return pltpu.make_async_copy(source[a].at[piece], target[a].at[piece], sem.at[i])

    for i in range(len(pieces)):
        step(arrays, held, i, in_sem).start()
    for i in range(len(pieces)):
        step(arrays, held, i, in_sem).wait()
        step(held, results, i, out_sem).start()
    for i in range(len(pieces)):
        step(held, results, i, out_sem).wait()


def build(mesh):
    n_dp, n_e = mesh.shape["dp"], mesh.shape["expert"]

    def body(
        tokens, memory, source_length, owner_device, source_device, target_length, routing,
        attn_gain, ffn_gain, query_weight, key_weight, value_weight, out_weight, router_weight,
        up_weight, down_weight, grad_out,
    ):
        sentences, length, width = tokens.shape
        z = Layout(
            n_dp, n_e, sentences, length, width, query_weight.shape[1], up_weight.shape[2],
            router_weight.shape[1],
        )
        T, D, F, R, H = z.T, z.D, z.F, z.R, z.H
        span = n_dp * TILE
        vm = pltpu.VMEM
        scratch = [
            vm((T, D), BF16), vm((T, F), BF16), vm((D, z.Hd), BF16), vm((D, z.Hd), BF16),
            vm((D, z.Hd), BF16), vm((z.Hd, D), BF16), vm((z.E, F), BF16), vm((D, H), BF16),
            vm((H, D), BF16),
            vm((n_e, T, F), BF16), vm((n_e, z.Hd, F), BF16), vm((n_e, T, z.Hd), BF16),
            vm((n_e, T, z.Hd), BF16), vm((n_e, T, z.Hd), BF16),
            vm((n_e, R, F), BF16), vm((n_e, R, F), BF16),
            vm((R, F), BF16), vm((R, F), BF16), vm((R, F), BF16), vm((R, F), BF16),
            vm((n_dp, LANES), F32),
            vm((2 * T, z.Hd), BF16), vm((span, z.Hd), BF16), vm((span, z.Hd), BF16),
            vm((2 * T, z.Hd), BF16),
            vm((2 * T, z.Hd), BF16), vm((span, z.Hd), BF16), vm((span, z.Hd), BF16),
            vm((2 * T, z.Hd), BF16),
            vm((n_e, 8, T), F32), vm((n_e, 8, T), F32), vm((n_e, z.E, T), F32),
            vm((z.E, LANES), F32), vm((n_dp, LANES), F32), vm((n_e, n_dp, LANES), F32),
            vm((n_dp, LANES), F32), vm((n_dp, LANES), F32),
            vm((R, T), BF16), vm((T, R), BF16), vm((T, R), BF16), vm((span, span), BF16),
            vm((R, H), F32), vm((R, H), BF16), vm((R, H), BF16),
            vm((4, R, F), BF16), vm((4, R, F), BF16), vm((R, F), F32), vm((R, F), F32),
            vm((3, R, F), BF16), vm((R, F), BF16), vm((3, R, F), BF16),
            vm((n_e, T, z.Hd), BF16), vm((n_e, T, z.Hd), BF16),
            vm((n_e, T, F), BF16), vm((n_e, T, F), BF16),
            vm((D, H), BF16), vm((H, D), BF16), vm((T, F), BF16), vm((T, F), F32),
            pltpu.SemaphoreType.DMA((SENDS,)), pltpu.SemaphoreType.DMA((SEMS,)),
            pltpu.SemaphoreType.DMA((16,)),
        ]
        smem = pl.BlockSpec(memory_space=pltpu.SMEM)
        vmem = pl.BlockSpec(memory_space=pltpu.VMEM)
        hbm = pl.BlockSpec(memory_space=pl.ANY)
        results = pl.pallas_call(
            functools.partial(layer_kernel, z),
            out_shape=(
                jax.ShapeDtypeStruct((T, F), BF16),
                jax.ShapeDtypeStruct((D, H), BF16),
                jax.ShapeDtypeStruct((H, D), BF16),
            ),
            in_specs=[smem] * 3 + [vmem] * 3 + [hbm] * 10,
            out_specs=(hbm, hbm, hbm),
            scratch_shapes=scratch,
            compiler_params=pltpu.CompilerParams(
                collective_id=0, has_side_effects=True, vmem_limit_bytes=56 * 1024 * 1024
            ),
            name="layer",
        )(
            source_device, source_length, target_length, jnp.transpose(routing, (0, 2, 1)),
            attn_gain[None], ffn_gain[None],
            tokens.reshape(T, D), memory.reshape(T, F), grad_out.reshape(T, D),
            query_weight, key_weight, value_weight, out_weight, router_weight.T,
            up_weight[0], down_weight[0],
        )
        mem_grad, up_grad, down_grad = pl.pallas_call(
            hand_on,
            out_shape=tuple(jax.ShapeDtypeStruct(r.shape, r.dtype) for r in results),
            in_specs=[hbm] * 3,
            out_specs=(hbm, hbm, hbm),
            scratch_shapes=[pltpu.VMEM(r.shape, r.dtype) for r in results]
            + [pltpu.SemaphoreType.DMA((17,)), pltpu.SemaphoreType.DMA((17,))],
            compiler_params=pltpu.CompilerParams(vmem_limit_bytes=56 * 1024 * 1024),
            name="hand_on",
        )(*results)
        return mem_grad.reshape(sentences, length, F), up_grad[None], down_grad[None]

    return body


def solution(mesh):
    in_specs = (
        P("dp", None, None),
        P("dp", None, "expert"),
        P("dp"),
        P("dp"),
        P("dp"),
        P("dp"),
        P("dp", None, None),
        P(),
        P(),
        P(None, "expert"),
        P(None, "expert"),
        P(None, "expert"),
        P("expert", None),
        P(),
        P("dp", None, "expert"),
        P("dp", "expert", None),
        P("dp", None, None),
    )
    out_specs = (P("dp", None, "expert"), P("dp", None, "expert"), P("dp", "expert", None))
    return jax.shard_map(
        build(mesh), mesh=mesh, in_specs=in_specs, out_specs=out_specs, check_vma=False
    )
```

```python
import functools

import jax
import jax.numpy as jnp
from jax import lax
from jax.experimental import pallas as pl
from jax.experimental.pallas import tpu as pltpu
from jax.sharding import PartitionSpec as P

F32 = jnp.float32
BF16 = jnp.bfloat16
HI = lax.Precision.HIGHEST
LANES = 128
CAP = 16
TILE = 16
GROUPS = 4
EPS = 1e-5


def dot(a, b, ca=1, cb=0, precision=None):
    return lax.dot_general(
        a, b, (((ca,), (cb,)), ((), ())), preferred_element_type=F32, precision=precision
    )


def iota(shape, dim):
    return lax.broadcasted_iota(jnp.int32, shape, dim)


def log2(value):
    return value.bit_length() - 1


def to_rows(columns):
    rows = columns[0].shape[0]
    lane = iota((rows, LANES), 1)
    packed = jnp.zeros((rows, LANES), F32)
    for i, column in enumerate(columns):
        packed = jnp.where(lane == i, column, packed)
    return packed.T[:8]


def to_columns(rows, count):
    padded = jnp.concatenate([rows, jnp.zeros((LANES - 8, rows.shape[1]), F32)], axis=0).T
    return [padded[:, i : i + 1] for i in range(count)]


def stack_rows(*rows):
    fill = jnp.zeros((8 - len(rows), rows[0].shape[1]), F32)
    return jnp.concatenate([*rows, fill], axis=0)


class Layout:
    def __init__(self, n_dp, n_e, sentences, length, width, head, hidden, experts):
        self.n_dp, self.n_e, self.n_x = n_dp, n_e, n_e // 2
        self.S, self.L, self.T = sentences, length, sentences * length
        self.D, self.F = width, width // n_e
        self.Hd, self.H, self.E = head, hidden, experts
        self.R = n_dp * CAP
        self.mids = n_dp // 2
        self.gs = n_dp // GROUPS
        self.Q = self.R // GROUPS


def layer_kernel(
    z,
    src_ref, slen_ref, tlen_ref, routing_ref, again_ref, fgain_ref,
    tokens_hbm, memory_hbm, grad_hbm, wq_hbm, wk_hbm, wv_hbm, wo_hbm, wr_hbm, up_hbm, down_hbm,
    mem_out, up_out, down_out,
    tok, live, wq, wk, wv, wo, wr, up, down,
    mem_all, ow_all, att_all, ag_send, ag_recv, x_all, g_all,
    g_send, x_send, ret_send, ret_recv,
    meta, kv_send, mid_buf, mid_out_buf, kv_recv, kvg_send, mid_buf2, mid_out2, kvg_recv,
    stat1, stat2, lg_all, gate_send, gate_recv, gg_all, gg_send, gg_recv,
    plan, plan0, plan1, relay_plan, u_buf, act_buf, pg_buf,
    sib_send, sib_recv, own_sum, held_sum, xs_send, far_recv, xs_recv, uw_send, uw_recv, mg_send, mg_recv,
    ug, dg, mg, hid,
    ss, rs, ls,
):
    n_dp, n_e, T, D, F, R, Q = z.n_dp, z.n_e, z.T, z.D, z.F, z.R, z.Q
    me = lax.axis_index("dp")
    e = lax.axis_index("expert")
    x, c = e // 2, e % 2
    xr, xl = (x + 1) % 4, (x + 3) % 4
    sib = 2 * x + (1 - c)
    right, left = 2 * xr + c, 2 * xl + c
    across = 2 * ((x + 2) % 4) + c
    my_group = me // z.gs
    col_e = pl.multiple_of(e * F, F)

    counter = [0, 0]

    def sems(count):
        first = counter[0]
        counter[0] += count
        return first

    def send_sem():
        counter[1] += 1
        return counter[1] - 1

    def copy(src, dst, ks, k, dp, ex):
        return pltpu.make_async_remote_copy(
            src_ref=src,
            dst_ref=dst,
            send_sem=ss.at[ks],
            recv_sem=rs.at[k],
            device_id=(dp, ex),
            device_id_type=pl.DeviceIdType.MESH,
        )

    pending = []

    def sent(ref, ks):
        copy(ref, ref, ks, 0, me, sib).wait_send()

    def sent_later(ref, ks):
        pending.append(lambda: sent(ref, ks))

    def arrive(dst, k):
        copy(dst, dst, 0, k, me, sib).wait_recv()

    def rows16(ref, i):
        return ref.at[pl.ds(pl.multiple_of(i * CAP, CAP), CAP)]

    def one_row(ref, i):
        return ref.at[pl.ds(i, 1)]

    def some16(ref):
        return lambda i, count: ref.at[pl.ds(pl.multiple_of(i * CAP, CAP), count * CAP)]

    def some_rows(ref):
        return lambda i, count: ref.at[pl.ds(i, count)]

    class Spread:
        def __init__(self, src, dst, some, by_group=False):
            self.src, self.dst, self.some, self.by_group = src, dst, some, by_group
            self.ks = send_sem()
            self.base = sems(GROUPS if by_group else 1)
            sent_later(some(0, n_dp - 1), self.ks)

        def start_group(self, group, k):
            arrival = self.base + (my_group if self.by_group else 0)

            def step(kk, carry):
                t = group * z.gs + (me % z.gs + kk) % z.gs
                copy(self.src(t), self.dst(me), self.ks, arrival, t, e).start()
                return carry

            lax.fori_loop(1 if k == 0 else 0, z.gs, step, 0)

        def start(self):
            for k in range(GROUPS):
                self.start_group((my_group + k) % GROUPS, k)

        def wait_group(self, group, k):
            count = z.gs - 1 if k == 0 else z.gs
            if count:
                arrive(self.some(group * z.gs, count), self.base + group)

        def wait(self):
            arrive(self.some(0, n_dp - 1), self.base)

    class Gather:
        def __init__(self, ref, first, rows, ringed=0):
            self.ref, self.first, self.rows, self.ringed = ref, first, rows, ringed
            self.parts = ref.shape[1] // rows
            self.ks = send_sem()
            self.base = sems(4 * self.parts)
            sent_later(ref.at[pl.ds(0, 7)], self.ks)

        def part(self, block, q):
            return self.ref.at[block, pl.ds(pl.multiple_of(self.first(q), TILE), self.rows)]

        def go(self, q, t, block, peer):
            ref = self.part(block, q)
            copy(ref, ref, self.ks, self.base + 4 * q + t, me, peer).start()

        def start(self, q):
            if q >= self.ringed:
                self.go(q, 2, e, across)
            self.go(q, 0, e, right)
            self.go(q, 1, e, left)
            self.go(q, 3, e, sib)

        def mid(self, q):
            for t, block, onward in ((0, left, right), (1, right, left)):
                arrive(self.part(block, q), self.base + 4 * q + t)
                if q < self.ringed and t == q % 2:
                    self.go(q, 2, block, onward)
                self.go(q, 3, block, sib)
            if q >= self.ringed:
                self.far(q)

        def far(self, q):
            arrive(self.part(across, q), self.base + 4 * q + 2)
            self.go(q, 3, across, sib)

        def end(self, q):
            four = self.ref.at[pl.ds(0, 4), pl.ds(pl.multiple_of(self.first(q), TILE), self.rows)]
            arrive(four, self.base + 4 * q + 3)

        def whole(self):
            for step in (self.start, self.mid, self.end):
                for q in range(self.parts):
                    step(q)

    class Exchange:
        def __init__(self, src, dst, ref):
            self.src, self.dst, self.ref = src, dst, ref
            self.ks = send_sem()
            self.base = sems(1)
            sent_later(ref.at[pl.ds(0, n_e - 1)], self.ks)

        def start(self, prepare=None):
            for p in (4, 5, 2, 3, 6, 7, 1):
                peer = 2 * ((x + p // 2) % 4) + (c + p % 2) % 2
                if prepare is not None:
                    prepare(peer)
                copy(self.src(peer), self.dst(e), self.ks, self.base, me, peer).start()

        def wait(self):
            arrive(self.ref.at[pl.ds(0, n_e - 1)], self.base)

    class Reduce:
        def __init__(self, first, n, partial, bufs, ring=None):
            self.n, self.partial, self.first, self.ring = n, partial, first, ring
            self.sib_send, self.sib_recv, self.own, self.held, self.xs, self.far, self.landing = bufs
            self.ks = send_sem()
            self.base = sems(6)
            sent_later(x_all.at[pl.ds(0, 7), pl.ds(0, n)], self.ks)

        def piece(self):
            return pl.ds(pl.multiple_of(self.first, TILE), self.n)

        def local(self):
            for dx in (2, 1, 3, 0):
                block = 2 * ((x + dx) % 4) + (1 - c)
                mine = self.sib_send.at[dx, self.piece()]
                mine[...] = self.partial(block).astype(BF16)
                theirs = self.sib_recv.at[dx, self.piece()]
                copy(mine, theirs, self.ks, self.base + dx, me, sib).start()

        def put(self, dx, value, landing, there, t):
            out = self.xs.at[dx - 1, self.piece()]
            out[...] = value.astype(BF16)
            copy(out, landing, self.ks, self.base + t, me, there).start()

        def pairs(self):
            waits = {None: None, 0: 1, 1: 3}[self.ring]
            for dx in (2, 1, 3, 0):
                there = 2 * ((x + dx) % 4) + c
                own = self.partial(there)
                theirs = self.sib_recv.at[dx, self.piece()]
                arrive(theirs, self.base + dx)
                both = own + theirs[...].astype(F32)
                if dx == 0:
                    self.own[self.piece(), :] = both
                elif dx == waits:
                    self.held[self.piece(), :] = both
                elif dx == 2 and self.ring is not None:
                    by = left if self.ring else right
                    self.put(dx, both, self.far.at[self.piece()], by, 5)
                else:
                    self.put(dx, both, self.landing.at[dx - 1, self.piece()], there, 4)

        def onward(self):
            dx, there = (3, left) if self.ring else (1, right)
            arrive(self.far.at[self.piece()], self.base + 5)
            both = self.held[self.piece(), :] + self.far[self.piece(), :].astype(F32)
            self.put(dx, both, self.landing.at[dx - 1, self.piece()], there, 4)

        def total(self):
            parts = (0, 1, 2) if self.ring is None else (0, 2)
            arrive(self.landing.at[pl.ds(0, len(parts)), self.piece()], self.base + 4)
            value = self.own[self.piece(), :]
            for i in parts:
                value = value + self.landing[i, self.piece(), :].astype(F32)
            return value

    def group(k):
        return (my_group + GROUPS - k) % GROUPS

    def group_first(k):
        return group(k) * Q

    local = {}

    def load(name, src, dst):
        copy_in = pltpu.make_async_copy(src, dst, ls.at[len(local)])
        copy_in.start()
        local[name] = copy_in

    load("memory", memory_hbm, mem_all.at[e])
    load("grad", grad_hbm.at[:, pl.ds(col_e, F)], live)
    load("wo", wo_hbm, wo)
    load("tokens", tokens_hbm, tok)
    load("wq", wq_hbm, wq)
    load("wk", wk_hbm, wk)
    load("wv", wv_hbm, wv)
    load("wr", wr_hbm.at[:, pl.ds(col_e, F)], wr)
    load("down", down_hbm, down)
    load("up", up_hbm, up)

    barrier = pltpu.get_barrier_semaphore()

    def greet(kk, carry):
        pl.semaphore_signal(
            barrier, inc=1, device_id=((me + kk) % n_dp, e), device_id_type=pl.DeviceIdType.MESH
        )
        return carry

    lax.fori_loop(1, n_dp, greet, 0)
    for p in range(1, n_e):
        pl.semaphore_signal(
            barrier, inc=1, device_id=(me, (e + p) % n_e), device_id_type=pl.DeviceIdType.MESH
        )

    choice_rows = jnp.concatenate([routing_ref[s] for s in range(z.S)], axis=1)
    expert_row = iota((z.E, T), 0)
    hot_rows = [expert_row == choice_rows[i : i + 1] for i in range(2)]
    hot = [h.astype(F32) for h in hot_rows]
    before = (iota((T, T), 0) < iota((T, T), 1)).astype(BF16)
    counts = dot((hot[0] + hot[1]).astype(BF16), before)
    rank_rows = [jnp.sum(h * counts, axis=0, keepdims=True) for h in hot]
    slot_rows = [choice_rows[i : i + 1].astype(F32) * CAP + rank_rows[i] for i in range(2)]
    rank0, rank1, slot0, slot1 = to_columns(stack_rows(*rank_rows, *slot_rows), 4)
    rank, slot = [rank0, rank1], [slot0, slot1]
    slot_row = iota((R, T), 0)
    plan[...] = jnp.logical_or(slot_row == slot_rows[0].astype(jnp.int32), slot_row == slot_rows[1].astype(jnp.int32)).astype(BF16)
    slot_lane = iota((T, R), 1)
    plan0[...] = (slot_lane == slot[0].astype(jnp.int32)).astype(BF16)
    plan1[...] = (slot_lane == slot[1].astype(jnp.int32)).astype(BF16)

    lane_1 = iota((1, LANES), 1)
    note = jnp.zeros((1, LANES), jnp.int32)
    for k in range(z.S):
        note = jnp.where(lane_1 == k, src_ref[k], note)
        note = jnp.where(lane_1 == z.S + k, slen_ref[k], note)
    meta[pl.ds(me, 1), :] = note.astype(F32)

    local["grad"].wait()
    row_t = iota((T, 1), 0)
    length = jnp.zeros((T, 1), jnp.int32)
    for k in range(z.S):
        length = jnp.where((row_t >> log2(z.L)) == k, tlen_ref[k], length)
    alive = (row_t & (z.L - 1)) < length
    live[...] = jnp.where(alive, live[...].astype(F32), 0.0).astype(BF16)
    slots = dot(plan[...], live[...]).astype(BF16)
    g_send[...] = slots
    own_rows = pl.ds(pl.multiple_of(me * CAP, CAP), CAP)
    g_all[e, own_rows, :] = g_send[own_rows, :]

    pl.semaphore_wait(barrier, n_dp - 1 + n_e - 1)

    local["memory"].wait()
    memory_gather = Gather(mem_all, lambda q: q * (T // 2), T // 2)
    memory_gather.start(0)
    memory_gather.start(1)
    meta_spread = Spread(lambda t: one_row(meta, me), lambda i: one_row(meta, i), some_rows(meta))
    meta_spread.start()
    g_spread = Spread(
        lambda t: rows16(g_send, t), lambda i: rows16(g_all.at[e], i), some16(g_all.at[e]), True
    )
    g_gather = Gather(g_all, group_first, Q)
    for k in range(2):
        g_spread.start_group((my_group + k) % GROUPS, k)

    local["tokens"].wait()
    local["wq"].wait()
    rows_f = tok[...].astype(F32)
    centred = rows_f - jnp.mean(rows_f, axis=1, keepdims=True)
    variance = jnp.mean(centred * centred, axis=1, keepdims=True)
    normed = (centred * lax.rsqrt(variance + EPS) * again_ref[...]).astype(BF16)
    queries = dot(normed, wq[...]).astype(BF16)

    local["wo"].wait()
    for b in range(n_e):

        @pl.when(e == b)
        def _():
            ow_all[b] = wo[:, b * F : (b + 1) * F]

    ow_exchange = Exchange(
        lambda peer: wo.at[:, pl.ds(pl.multiple_of(peer * F, F), F)],
        lambda b: ow_all.at[b],
        ow_all,
    )
    for q in range(2):
        memory_gather.mid(q)
    for q in range(2):
        memory_gather.end(q)
    ow_exchange.start()

    local["wk"].wait()
    local["wv"].wait()
    keys = jnp.zeros((T, z.Hd), F32)
    values = jnp.zeros((T, z.Hd), F32)
    for b in range(n_e):
        block = mem_all[b]
        keys = keys + dot(block, wk[b * F : (b + 1) * F, :])
        values = values + dot(block, wv[b * F : (b + 1) * F, :])

    r_out = iota((2 * T, 2 * T), 0)
    r_in = iota((2 * T, 2 * T), 1)
    place = (
        ((r_out >> 3) & 1) * T + ((r_out >> 1) & 3) * z.L + ((r_out >> 4) << 1) + (r_out & 1)
    )
    order = (r_in == place).astype(BF16)

    middle_me = me % 2 == (me // 4 + c) % 2
    my_middle = me // 2

    def middle_dp(m):
        return 2 * m + (m // 2 + c) % 2

    class Relay:
        def __init__(self, send_buf, held, sorted_buf, recv_buf):
            self.send_buf, self.held, self.sorted_buf, self.recv_buf = (
                send_buf, held, sorted_buf, recv_buf,
            )
            self.out, self.back = sems(1), sems(1)
            self.ks_out, self.ks_back = send_sem(), send_sem()

        def each_middle(self, action):
            def step(kk, carry):
                m = (my_middle + kk) % z.mids

                @pl.when(middle_dp(m) != me)
                def _():
                    action(m)

                return carry

            lax.fori_loop(0, z.mids, step, 0)

        def first(self, m):
            copy(
                rows16(self.send_buf, m), rows16(self.held, me), self.ks_out, self.out,
                middle_dp(m), e,
            ).start()

        def start(self):
            self.each_middle(self.first)

            @pl.when(middle_me)
            def _():
                rows16(self.held, me)[...] = rows16(self.send_buf, my_middle)[...]

        def turn(self, transposed):
            @pl.when(middle_me)
            def _():
                arrive(some16(self.held)(0, n_dp - 1), self.out)
                self.sorted_buf[...] = dot(
                    relay_plan[...], self.held[...], 0 if transposed else 1, 0
                ).astype(BF16)

                def step(kk, carry):
                    j = (me + kk) % n_dp
                    copy(
                        rows16(self.sorted_buf, j), rows16(self.recv_buf, my_middle),
                        self.ks_back, self.back, j, e,
                    ).start()
                    return carry

                lax.fori_loop(1, n_dp, step, 0)
                rows16(self.recv_buf, my_middle)[...] = rows16(self.sorted_buf, me)[...]

        def end(self):
            @pl.when(middle_me)
            def _():
                arrive(some16(self.recv_buf)(0, z.mids - 1), self.back)

            @pl.when(jnp.logical_not(middle_me))
            def _():
                arrive(self.recv_buf, self.back)

        def finish(self):
            @pl.when(middle_me)
            def _():
                sent(some16(self.send_buf)(0, z.mids - 1), self.ks_out)
                sent(some16(self.sorted_buf)(0, n_dp - 1), self.ks_back)

            @pl.when(jnp.logical_not(middle_me))
            def _():
                sent(self.send_buf, self.ks_out)

    both = jnp.concatenate([keys.astype(BF16), values.astype(BF16)], axis=0)
    kv_send[...] = dot(order, both).astype(BF16)
    relay = Relay(kv_send, mid_buf, mid_out_buf, kv_recv)
    relay.start()

    meta_spread.wait()
    notes = meta[...]
    span = n_dp * TILE
    pick = ((iota((span, n_dp), 0) >> 4) == iota((span, n_dp), 1)).astype(BF16)
    spread_notes = dot(pick, notes.astype(BF16))
    wanted = ((iota((span, LANES), 0) >> 1) & 3) == iota((span, LANES), 1)
    source = jnp.sum(jnp.where(wanted, spread_notes, 0.0), axis=1, keepdims=True).astype(jnp.int32)
    p_row = iota((span, span), 0)
    p_col = iota((span, span), 1)
    relay_plan[...] = (p_col == (source * TILE + (p_row & (TILE - 1)))).astype(BF16)
    for k in range(2):
        g_spread.wait_group(group(k), k)
        g_gather.start(k)
    relay.turn(False)
    for k in range(2, GROUPS):
        g_spread.start_group((my_group + k) % GROUPS, k)
    g_gather.mid(0)

    key_length = jnp.zeros((1, T), F32)
    key_at = iota((1, T), 1)
    n_row, n_lane = iota((n_dp, LANES), 0), iota((n_dp, LANES), 1)
    for k in range(z.S):
        here = jnp.logical_and(n_row == src_ref[k], n_lane == z.S + k)
        found = jnp.sum(jnp.where(here, notes, 0.0), axis=1, keepdims=True)
        found = jnp.sum(found, axis=0, keepdims=True)
        key_length = jnp.where((key_at >> log2(z.L)) == k, found, key_length)

    relay.end()
    kv = dot(order, kv_recv[...], 0, 0).astype(BF16)
    key_heads, value_heads = kv[:T], kv[T:]

    scaling = z.Hd ** (-0.5)
    same = (iota((T, T), 0) >> log2(z.L)) == (iota((T, T), 1) >> log2(z.L))
    inside = (key_at & (z.L - 1)).astype(F32) < key_length
    open_keys = jnp.logical_and(same, inside)
    scores = jnp.where(open_keys, dot(queries, key_heads, 1, 1) * scaling, -1e30)
    exps = jnp.exp(scores - jnp.max(scores, axis=1, keepdims=True))
    probabilities = exps / jnp.sum(exps, axis=1, keepdims=True)
    weights = probabilities.astype(BF16)
    att_all[e] = dot(weights, value_heads).astype(BF16)
    att_gather = Gather(att_all, lambda q: 0, T)
    att_gather.start(0)
    g_gather.mid(1)
    g_spread.wait_group(group(2), 2)
    g_gather.start(2)
    att_gather.mid(0)
    ow_exchange.wait()
    att_gather.end(0)

    heads_sum = jnp.zeros((T, F), F32)
    for b in range(n_e):
        heads_sum = heads_sum + dot(att_all[b], ow_all[b])
    hidden = (tok[:, pl.ds(col_e, F)].astype(F32) + heads_sum).astype(BF16).astype(F32)
    hid[...] = hidden
    part_sum = jnp.sum(hidden, axis=1, keepdims=True)
    off = hidden - part_sum * (1.0 / F)
    part_sq = jnp.sum(off * off, axis=1, keepdims=True)
    stat1[e] = to_rows([part_sum, part_sq])
    stat1_exchange = Exchange(lambda peer: stat1.at[e], lambda b: stat1.at[b], stat1)
    stat1_exchange.start()
    g_gather.mid(2)
    stat1_exchange.wait()
    g_spread.wait_group(group(3), 3)
    g_gather.start(3)
    parts = [stat1[b] for b in range(n_e)]
    mean_row = sum(p[0:1] for p in parts) * (1.0 / D)
    square_row = sum(p[1:2] for p in parts)
    for p in parts:
        shift = p[0:1] * (1.0 / F) - mean_row
        square_row = square_row + F * (shift * shift)
    rstd_row = lax.rsqrt(square_row * (1.0 / D) + EPS)
    mean, rstd = to_columns(stack_rows(mean_row, rstd_row), 2)
    gain = fgain_ref[:, pl.ds(col_e, F)]
    unit = (hidden - mean) * rstd
    expert_in = (unit * gain).astype(BF16)

    x_send[...] = dot(plan[...], expert_in).astype(BF16)
    x_all[e, own_rows, :] = x_send[own_rows, :]
    x_spread = Spread(
        lambda t: rows16(x_send, t), lambda i: rows16(x_all.at[e], i), some16(x_all.at[e]), True
    )
    x_spread.start()
    local["wr"].wait()
    router = wr[...]
    lg_all[e] = dot(router, expert_in, 1, 1)
    lg_exchange = Exchange(lambda peer: lg_all.at[e], lambda b: lg_all.at[b], lg_all)
    lg_exchange.start()

    local["down"].wait()

    def down_back(k):
        piece = pl.ds(pl.multiple_of(group_first(k), Q), Q)
        total = jnp.zeros((Q, z.H), F32)
        for b in range(n_e):
            total = total + dot(g_all[b, piece, :], down[:, b * F : (b + 1) * F], 1, 1)
        u_buf[piece, :] = total

    x_gather = Gather(x_all, group_first, Q, 0)

    def x_start(k):
        x_spread.wait_group(group(k), k)
        x_gather.start(k)

    g_gather.end(0)
    down_back(0)
    x_start(0)
    g_gather.end(1)
    down_back(1)
    x_start(1)

    lg_exchange.wait()
    logits = sum(lg_all[b] for b in range(n_e))
    chosen = [jnp.sum(jnp.where(h, logits, 0.0), axis=0, keepdims=True) for h in hot_rows]
    top = jnp.maximum(chosen[0], chosen[1])
    lifted = [jnp.exp(v - top) for v in chosen]
    share = [v / (lifted[0] + lifted[1]) for v in lifted]
    rank_lane = [
        (iota((T, LANES), 1) == rank[i].astype(jnp.int32)).astype(F32) for i in range(2)
    ]
    gate_rows = jnp.zeros((z.E, LANES), F32)
    for i in range(2):
        gate_rows = gate_rows + dot(jnp.where(hot_rows[i], share[i], 0.0), rank_lane[i], 1, 0, HI)
    gate_send[...] = gate_rows
    gate_recv[pl.ds(me, 1), :] = gate_send[pl.ds(me, 1), :]
    gate_spread = Spread(
        lambda t: one_row(gate_send, t), lambda i: one_row(gate_recv, i), some_rows(gate_recv)
    )
    gate_spread.start()
    g_gather.mid(3)
    g_gather.end(2)
    down_back(2)
    x_start(2)
    g_gather.end(3)
    down_back(3)
    x_start(3)

    local["up"].wait()
    reduces = []

    def expert_group(k):
        first = group_first(k)
        piece = pl.ds(pl.multiple_of(first, Q), Q)
        pre = jnp.zeros((Q, z.H), F32)
        for b in range(n_e):
            pre = pre + dot(x_all[b, piece, :], up[b * F : (b + 1) * F, :])
        cubic = pre * pre * pre
        slope_in = 0.7978845608028654 * (pre + 0.044715 * cubic)
        bend = jnp.tanh(slope_in)
        act = (pre * (0.5 * (1.0 + bend))).astype(BF16)
        act_buf[piece, :] = act
        slope = 0.5 * (1.0 + bend) + 0.5 * pre * (1.0 - bend * bend) * (
            0.7978845608028654 * (1.0 + 3.0 * 0.044715 * pre * pre)
        )
        grads = u_buf[piece, :]
        steep = grads * slope
        u_buf[piece, :] = steep
        pg_buf[piece, :] = steep.astype(BF16)
        pick, wanted = slot_masks(first, Q)
        dots = jnp.sum(act.astype(F32) * grads, axis=1, keepdims=True)
        return dot(pick, jnp.where(wanted, dots, 0.0), 0, 0, HI)

    def slot_masks(first, rows):
        pick = (((iota((rows, n_dp), 0) + first) >> 4) == iota((rows, n_dp), 1)).astype(F32)
        wanted = (iota((rows, LANES), 0) & (CAP - 1)) == iota((rows, LANES), 1)
        return pick, wanted

    def input_partial(first):
        def partial(block):
            piece = pl.ds(pl.multiple_of(first, Q), Q)
            rows = pl.ds(pl.multiple_of(block * F, F), F)
            return dot(pg_buf[piece, :], up[rows, :], 1, 1)

        return partial

    ret_spread = Spread(
        lambda t: rows16(ret_send, t), lambda i: rows16(ret_recv, i), some16(ret_recv)
    )
    bufs = (sib_send, sib_recv, own_sum, held_sum, xs_send, far_recv, xs_recv)

    def give_back(k):
        first = group_first(k)
        piece = pl.ds(pl.multiple_of(first, Q), Q)
        ret_send[piece, :] = reduces[k].total().astype(BF16)
        ret_spread.start_group(group(k), k)

    gg_total = jnp.zeros((n_dp, LANES), F32)
    x_gather.mid(0)
    for k in range(GROUPS):
        if k + 1 < GROUPS:
            x_gather.mid(k + 1)
        x_gather.end(k)
        gg_total = gg_total + expert_group(k)
        if k == GROUPS - 1:
            gg_all[e] = gg_total
            gg_exchange = Exchange(lambda peer: gg_all.at[e], lambda b: gg_all.at[b], gg_all)
            gg_exchange.start()
        reduces.append(
            Reduce(group_first(k), Q, input_partial(group_first(k)), bufs, None)
        )
        reduces[k].local()
        reduces[k].pairs()

    def up_back(b, carry):
        rows = pl.ds(pl.multiple_of(b * F, F), F)
        ug[rows, :] = dot(x_all[b], pg_buf[...], 0, 0).astype(BF16)
        return carry

    pick, wanted = slot_masks(0, R)
    gate_spread.wait()
    spread_gates = dot(pick, gate_recv[...], 1, 0, HI)
    gates_all = jnp.sum(jnp.where(wanted, spread_gates, 0.0), axis=1, keepdims=True)

    def down_grad(b, carry):
        columns = pl.ds(pl.multiple_of(b * F, F), F)
        scaled = (g_all[b].astype(F32) * gates_all).astype(BF16)
        dg[:, columns] = dot(act_buf[...], scaled, 0, 0).astype(BF16)
        return carry

    give_back(0)
    gg_exchange.wait()
    gg_sum = sum(gg_all[b] for b in range(n_e))
    gg_send[...] = gg_sum
    gg_recv[pl.ds(me, 1), :] = gg_send[pl.ds(me, 1), :]
    gg_spread = Spread(
        lambda t: one_row(gg_send, t), lambda i: one_row(gg_recv, i), some_rows(gg_recv)
    )
    gg_spread.start()
    give_back(1)
    pg_buf[...] = (gates_all * u_buf[...]).astype(BF16)
    lax.fori_loop(0, n_e // 2, up_back, 0)
    give_back(2)
    lax.fori_loop(n_e // 2, n_e, up_back, 0)
    give_back(3)
    ret_recv[own_rows, :] = ret_send[own_rows, :]

    unit_bf = ((hid[...] - mean) * rstd).astype(BF16)

    def unit_part(head):
        uw_send[head] = dot(unit_bf, ow_all[head], 1, 1).astype(BF16)

    uw_exchange = Exchange(lambda peer: uw_send.at[peer], lambda b: uw_recv.at[b], uw_recv)
    uw_exchange.start(unit_part)
    uw_recv[e] = dot(unit_bf, ow_all[e], 1, 1).astype(BF16)

    up_store = pltpu.make_async_copy(ug, up_out, ls.at[len(local)])
    up_store.start()
    lax.fori_loop(0, n_e // 2, down_grad, 0)

    gg_spread.wait()
    gate_grad = []
    for i in range(2):
        spread_gg = dot(gg_recv[...], rank_lane[i], 1, 1, HI)
        gate_grad.append(jnp.sum(jnp.where(hot_rows[i], spread_gg, 0.0), axis=0, keepdims=True))
    delta = share[0] * share[1] * (gate_grad[0] - gate_grad[1])
    logit_grad = jnp.where(hot_rows[0], delta, 0.0) - jnp.where(hot_rows[1], delta, 0.0)
    high = logit_grad.astype(BF16)
    low = (logit_grad - high.astype(F32)).astype(BF16)
    router_term = dot(high, router, 0, 0) + dot(low, router, 0, 0)
    share_columns = to_columns(stack_rows(share[0], share[1]), 2)

    ret_spread.wait()
    returned = ret_recv[...]
    ffn_in_grad = (
        (share_columns[0] * share_columns[0]) * dot(plan0[...], returned)
        + (share_columns[1] * share_columns[1]) * dot(plan1[...], returned)
        + router_term
    )

    scaled_in = ffn_in_grad * gain
    unit = (hid[...] - mean) * rstd
    stat2[e] = to_rows(
        [
            jnp.sum(scaled_in, axis=1, keepdims=True),
            jnp.sum(scaled_in * unit, axis=1, keepdims=True),
        ]
    )
    stat2_exchange = Exchange(lambda peer: stat2.at[e], lambda b: stat2.at[b], stat2)
    stat2_exchange.start()
    sent_grad = (live[...].astype(F32) + rstd * scaled_in).astype(BF16)

    def head_part(head):
        ag_send[head] = dot(sent_grad, ow_all[head], 1, 1).astype(BF16)

    ag_exchange = Exchange(lambda peer: ag_send.at[peer], lambda b: ag_recv.at[b], ag_recv)
    ag_exchange.start(head_part)
    ag_recv[e] = jnp.zeros((T, z.Hd), BF16)
    att_grad = dot(sent_grad, ow_all[e], 1, 1)
    lax.fori_loop(n_e // 2, n_e, down_grad, 0)
    down_store = pltpu.make_async_copy(dg, down_out, ls.at[len(local) + 1])
    down_store.start()
    uw_exchange.wait()
    unit_heads = sum(uw_recv[b].astype(F32) for b in range(n_e))
    weight_sums = dot(jnp.ones((8, D), BF16), wo[...], 1, 1)[:1]
    stat2_exchange.wait()
    sums = sum(stat2[b] for b in range(n_e)) * (1.0 / D)
    mean_in, mean_unit = to_columns(sums, 2)
    ag_exchange.wait()

    att_grad = att_grad + sum(ag_recv[b].astype(F32) for b in range(n_e))
    att_grad = att_grad - (rstd * mean_in) * weight_sums - (rstd * mean_unit) * unit_heads
    att_grad = att_grad.astype(BF16)
    value_grad = dot(weights, att_grad, 0, 0).astype(BF16)
    prob_grad = dot(att_grad, value_heads, 1, 1)
    inner = jnp.sum(probabilities * prob_grad, axis=1, keepdims=True)
    score_grad = (probabilities * (prob_grad - inner) * scaling).astype(BF16)
    key_grad = dot(score_grad, queries, 0, 0).astype(BF16)
    both = jnp.concatenate([key_grad, value_grad], axis=0)
    kvg_send[...] = dot(order, both).astype(BF16)
    relay_back = Relay(kvg_send, mid_buf2, mid_out2, kvg_recv)
    relay_back.start()
    relay_back.turn(True)
    relay_back.end()
    home = dot(order, kvg_recv[...], 0, 0).astype(BF16)
    home_keys, home_values = home[:T], home[T:]

    def memory_partial(block):
        rows = pl.ds(pl.multiple_of(block * F, F), F)
        return dot(home_keys, wk[rows, :], 1, 1) + dot(home_values, wv[rows, :], 1, 1)

    def memory_send(block):
        mg_send[block] = memory_partial(block).astype(BF16)

    memory_exchange = Exchange(lambda peer: mg_send.at[peer], lambda b: mg_recv.at[b], mg_recv)
    memory_exchange.start(memory_send)
    mg_recv[e] = jnp.zeros((T, F), BF16)
    own_part = memory_partial(e)
    memory_exchange.wait()
    mg[...] = (own_part + sum(mg_recv[b].astype(F32) for b in range(n_e))).astype(BF16)
    mem_store = pltpu.make_async_copy(mg, mem_out, ls.at[len(local) + 2])
    mem_store.start()

    relay.finish()
    relay_back.finish()
    for finish in pending:
        finish()
    up_store.wait()
    down_store.wait()
    mem_store.wait()
    assert counter[0] <= SEMS and counter[1] <= SENDS, counter


SEMS = 96
SENDS = 32


def hand_on(*refs):
    arrays, results, held = refs[0:3], refs[3:6], refs[6:9]
    in_sem, out_sem = refs[9:]
    pieces = []
    for a in range(3):
        rows = arrays[a].shape[0]
        cuts = 8 if rows >= 512 else 1
        for j in range(cuts):
            pieces.append((a, pl.ds(j * (rows // cuts), rows // cuts)))

    def step(source, target, i, sem):
        a, piece = pieces[i]
        return pltpu.make_async_copy(source[a].at[piece], target[a].at[piece], sem.at[i])

    for i in range(len(pieces)):
        step(arrays, held, i, in_sem).start()
    for i in range(len(pieces)):
        step(arrays, held, i, in_sem).wait()
        step(held, results, i, out_sem).start()
    for i in range(len(pieces)):
        step(held, results, i, out_sem).wait()


def build(mesh):
    n_dp, n_e = mesh.shape["dp"], mesh.shape["expert"]

    def body(
        tokens, memory, source_length, owner_device, source_device, target_length, routing,
        attn_gain, ffn_gain, query_weight, key_weight, value_weight, out_weight, router_weight,
        up_weight, down_weight, grad_out,
    ):
        sentences, length, width = tokens.shape
        z = Layout(
            n_dp, n_e, sentences, length, width, query_weight.shape[1], up_weight.shape[2],
            router_weight.shape[1],
        )
        T, D, F, R, H = z.T, z.D, z.F, z.R, z.H
        span = n_dp * TILE
        vm = pltpu.VMEM
        scratch = [
            vm((T, D), BF16), vm((T, F), BF16), vm((D, z.Hd), BF16), vm((D, z.Hd), BF16),
            vm((D, z.Hd), BF16), vm((z.Hd, D), BF16), vm((z.E, F), BF16), vm((D, H), BF16),
            vm((H, D), BF16),
            vm((n_e, T, F), BF16), vm((n_e, z.Hd, F), BF16), vm((n_e, T, z.Hd), BF16),
            vm((n_e, T, z.Hd), BF16), vm((n_e, T, z.Hd), BF16),
            vm((n_e, R, F), BF16), vm((n_e, R, F), BF16),
            vm((R, F), BF16), vm((R, F), BF16), vm((R, F), BF16), vm((R, F), BF16),
            vm((n_dp, LANES), F32),
            vm((2 * T, z.Hd), BF16), vm((span, z.Hd), BF16), vm((span, z.Hd), BF16),
            vm((2 * T, z.Hd), BF16),
            vm((2 * T, z.Hd), BF16), vm((span, z.Hd), BF16), vm((span, z.Hd), BF16),
            vm((2 * T, z.Hd), BF16),
            vm((n_e, 8, T), F32), vm((n_e, 8, T), F32), vm((n_e, z.E, T), F32),
            vm((z.E, LANES), F32), vm((n_dp, LANES), F32), vm((n_e, n_dp, LANES), F32),
            vm((n_dp, LANES), F32), vm((n_dp, LANES), F32),
            vm((R, T), BF16), vm((T, R), BF16), vm((T, R), BF16), vm((span, span), BF16),
            vm((R, H), F32), vm((R, H), BF16), vm((R, H), BF16),
            vm((4, R, F), BF16), vm((4, R, F), BF16), vm((R, F), F32), vm((R, F), F32),
            vm((3, R, F), BF16), vm((R, F), BF16), vm((3, R, F), BF16),
            vm((n_e, T, z.Hd), BF16), vm((n_e, T, z.Hd), BF16),
            vm((n_e, T, F), BF16), vm((n_e, T, F), BF16),
            vm((D, H), BF16), vm((H, D), BF16), vm((T, F), BF16), vm((T, F), F32),
            pltpu.SemaphoreType.DMA((SENDS,)), pltpu.SemaphoreType.DMA((SEMS,)),
            pltpu.SemaphoreType.DMA((16,)),
        ]
        smem = pl.BlockSpec(memory_space=pltpu.SMEM)
        vmem = pl.BlockSpec(memory_space=pltpu.VMEM)
        hbm = pl.BlockSpec(memory_space=pl.ANY)
        results = pl.pallas_call(
            functools.partial(layer_kernel, z),
            out_shape=(
                jax.ShapeDtypeStruct((T, F), BF16),
                jax.ShapeDtypeStruct((D, H), BF16),
                jax.ShapeDtypeStruct((H, D), BF16),
            ),
            in_specs=[smem] * 3 + [vmem] * 3 + [hbm] * 10,
            out_specs=(hbm, hbm, hbm),
            scratch_shapes=scratch,
            compiler_params=pltpu.CompilerParams(
                collective_id=0, has_side_effects=True, vmem_limit_bytes=56 * 1024 * 1024
            ),
            name="layer",
        )(
            source_device, source_length, target_length, jnp.transpose(routing, (0, 2, 1)),
            attn_gain[None], ffn_gain[None],
            tokens.reshape(T, D), memory.reshape(T, F), grad_out.reshape(T, D),
            query_weight, key_weight, value_weight, out_weight, router_weight.T,
            up_weight[0], down_weight[0],
        )
        mem_grad, up_grad, down_grad = pl.pallas_call(
            hand_on,
            out_shape=tuple(jax.ShapeDtypeStruct(r.shape, r.dtype) for r in results),
            in_specs=[hbm] * 3,
            out_specs=(hbm, hbm, hbm),
            scratch_shapes=[pltpu.VMEM(r.shape, r.dtype) for r in results]
            + [pltpu.SemaphoreType.DMA((17,)), pltpu.SemaphoreType.DMA((17,))],
            compiler_params=pltpu.CompilerParams(vmem_limit_bytes=56 * 1024 * 1024),
            name="hand_on",
        )(*results)
        return mem_grad.reshape(sentences, length, F), up_grad[None], down_grad[None]

    return body


def solution(mesh):
    in_specs = (
        P("dp", None, None),
        P("dp", None, "expert"),
        P("dp"),
        P("dp"),
        P("dp"),
        P("dp"),
        P("dp", None, None),
        P(),
        P(),
        P(None, "expert"),
        P(None, "expert"),
        P(None, "expert"),
        P("expert", None),
        P(),
        P("dp", None, "expert"),
        P("dp", "expert", None),
        P("dp", None, None),
    )
    out_specs = (P("dp", None, "expert"), P("dp", None, "expert"), P("dp", "expert", None))
    return jax.shard_map(
        build(mesh), mesh=mesh, in_specs=in_specs, out_specs=out_specs, check_vma=False
    )
```
